32 devices in a mesh: run: 2 (over core), row: 4 (over y, x), col: 4 (over z).
Axes of the slice: x: 2, y: 2, z: 4, core: 2. Of those that a mesh axis runs over, the one named last changes fastest.
Arguments:
- init_field: float32 [96, 256, 512], P('run', 'row', 'col'), may hold values from -6 to 6
- conduct: float32 [256, 512], P('row', 'col'), may hold values from 0.5 to 2
- nonlin: float32 [96], P('run'), may hold values from 0.1 to 1
- counts: int32 [96], P('run'), may hold values from 1 to 8
- descriptors: bfloat16 [96, 256], replicated, may hold values from -6 to 6
- time_code: bfloat16 [8, 256], replicated, may hold values from -6 to 6
- w_in: bfloat16 [256, 512], replicated, may hold values from -0.375 to 0.375
- bias_in: float32 [512], replicated, may hold values from -6 to 6
- w_out: bfloat16 [512, 512], replicated, may hold values from -0.25 to 0.25
- decoder: bfloat16 [512, 256, 512], P(None, ('row', 'col')), may hold values from -0.22 to 0.22
Outputs:
- final_field: float32 [96, 256, 512], P('run', 'row', 'col')
- new_w_in: float32 [256, 512], replicated
- new_bias: float32 [512], replicated
- new_w_out: float32 [512, 512], replicated
- mean_loss: float32 [], replicated
The draws below stay inside these ranges and needn't reach their ends.
All inputs are finite; a program needn't handle non-finite values.
Results may differ from the reference program's by a relative error of at most 0.0017.
Values may be sent and summed in bfloat16 or wider, within the bound.
No kernel may reach another device: no remote copies, remote signals or barrier semaphores. Data moves between devices by JAX's collectives and lax.ppermute only.
A program may use at most 128 MiB of HBM per device.

```python
import math
import jax
import jax.numpy as jnp
from jax import lax

P_SIZE = 256
H = 512
STEPS = 8
RUNS = 96
GRID_ROWS = 256
GRID_COLS = 512


pattern_count = 8


def smooth_patterns(key):
    freq_key = jax.random.fold_in(key, 3)
    phase_key = jax.random.fold_in(key, 5)
    frequency = jax.random.randint(freq_key, (pattern_count, 2), 1, 4).astype(jnp.float32)
    phase_draw = jax.random.uniform(phase_key, (pattern_count, 2), jnp.float32, 0.0, 2.0 * math.pi)
    row_place = jnp.arange(GRID_ROWS, dtype=jnp.float32) / GRID_ROWS
    col_place = jnp.arange(GRID_COLS, dtype=jnp.float32) / GRID_COLS
    along_rows = jnp.cos(2.0 * math.pi * frequency[:, 0:1] * row_place[None, :] + phase_draw[:, 0:1])
    along_cols = jnp.cos(2.0 * math.pi * frequency[:, 1:2] * col_place[None, :] + phase_draw[:, 1:2])
    return 2.0 * along_rows[:, :, None] * along_cols[:, None, :]


def draw_init_field(key, part):
    shapes = smooth_patterns(jax.random.fold_in(key, 7))
    coef_key = jax.random.fold_in(key, 11)
    rough_key = jax.random.fold_in(key, 13)
    weights_mix = 0.5 * jax.random.normal(coef_key, (RUNS, pattern_count), jnp.float32)
    rough = jax.random.normal(rough_key, (RUNS, GRID_ROWS, GRID_COLS), jnp.float32)
    smooth = jnp.einsum('rk,kij->rij', weights_mix, shapes)
    return jnp.clip(smooth + rough, -6.0, 6.0)


def draw_decoder(key, part):
    shapes = smooth_patterns(jax.random.fold_in(key, 7))
    mix_key = jax.random.fold_in(key, 17)
    noise_key = jax.random.fold_in(key, 19)
    noise = jax.random.normal(noise_key, (H, GRID_ROWS, GRID_COLS), jnp.float32)
    blend = 0.002
    mixing = jax.random.normal(mix_key, (H, pattern_count), jnp.float32)
    smooth = jnp.einsum('hk,kij->hij', mixing, shapes)
    return jnp.clip(noise * H ** (-0.5) + blend * smooth, -0.22, 0.22).astype(jnp.bfloat16)


def set_ends(values, rng, least, largest):
    longest = values.shape.index(max(values.shape))
    spots = []
    for shift in (0, 1):
        where = [jax.random.randint(jax.random.fold_in(rng, axis), (), 0, length) for axis, length in enumerate(values.shape)]
        where[longest] = (where[longest] + shift) % values.shape[longest]
        spots.append(tuple(where))
    return values.at[spots[0]].set(least).at[spots[1]].set(largest)


def block_levels(rng, extent, shards, smallest, high):
    def one(position, shards_of):
        draws = jax.random.uniform(jax.random.fold_in(jax.random.fold_in(rng, 6), position), (shards_of,), jnp.float32, smallest / len(shards), high / len(shards))
        return jnp.repeat(jnp.exp(draws), extent[position] // shards_of).reshape((-1,) + (1,) * (len(extent) - position - 1))

    loudness = one(*shards[0])
    for cut in shards[1:]:
        loudness = loudness * one(*cut)
    return loudness


def centred(rng, dims, scale, reach, kind=jnp.bfloat16):
    return jnp.clip(scale * jax.random.normal(rng, dims, jnp.float32), -reach, reach).astype(kind)


def setup_inputs(seed: int = 0) -> dict:
    key_list = jax.random.split(jax.random.key(seed), 11)
    init_field = draw_init_field(jax.random.fold_in(key_list[10], 71), 0)
    conduct = jnp.clip(jnp.exp(math.log(2.0) - 1.3862944 * jax.random.uniform(key_list[1], (GRID_ROWS, GRID_COLS), jnp.float32) ** block_levels(key_list[1], (GRID_ROWS, GRID_COLS), ((0, 4), (1, 4)), -0.2, 0.2)), 0.5, 2.0)
    nonlin = jnp.clip(jnp.exp(math.log(1.0) - 2.3025851 * jax.random.uniform(key_list[2], (RUNS,), jnp.float32) ** block_levels(key_list[2], (RUNS,), ((0, 2),), -0.2, 0.2)), 0.1, 1.0)
    counts = set_ends(jax.random.randint(key_list[3], (RUNS,), 1, STEPS + 1), jax.random.fold_in(key_list[3], 1), 1, STEPS).astype(jnp.int32)
    descriptors = centred(key_list[4], (RUNS, P_SIZE), 1.0, 6.0)
    time_code = centred(key_list[5], (STEPS, P_SIZE), 1.0, 6.0)
    w_in = centred(key_list[6], (P_SIZE, H), P_SIZE ** -0.5, 0.375)
    bias_in = centred(key_list[7], (H,), 1.0, 6.0, jnp.float32)
    w_out = centred(key_list[8], (H, H), H ** -0.5, 0.25)
    decoder = draw_decoder(jax.random.fold_in(key_list[10], 71), 0)
    return {"init_field": init_field, "conduct": conduct, "nonlin": nonlin, "counts": counts, "descriptors": descriptors, "time_code": time_code, "w_in": w_in, "bias_in": bias_in, "w_out": w_out, "decoder": decoder}


time_step = 0.12
learn_rate = 0.5

def advance(padded, cond_pad, nonlin, active, inside):
    kappa = cond_pad[None] / (1.0 + nonlin[:, None, None] * padded * padded)
    centre = padded[:, 1:-1, 1:-1]
    middle = kappa[:, 1:-1, 1:-1]
    flux = jnp.zeros_like(centre)
    places = ((slice(2, None), slice(1, -1)), (slice(0, -2), slice(1, -1)), (slice(1, -1), slice(2, None)), (slice(1, -1), slice(0, -2)))
    for rows_at, cols_at in places:
        flux = flux + 0.5 * (middle + kappa[:, rows_at, cols_at]) * (padded[:, rows_at, cols_at] - centre)
    moved = jnp.where(inside[None, 1:-1, 1:-1], centre + time_step * flux, jnp.zeros_like(centre))
    return jnp.where(active[:, None, None], moved, centre)

def trunk(rows_in, w_in, bias_in, w_out):
    pre = jnp.dot(rows_in, w_in, preferred_element_type=jnp.float32) + bias_in
    act = jax.nn.gelu(pre).astype(jnp.bfloat16)
    hidden = jnp.dot(act, w_out, preferred_element_type=jnp.float32).astype(jnp.bfloat16)
    return (pre, act, hidden)

def trunk_grads(rows_in, pre, act, w_out, dhidden):
    grad_b = dhidden.astype(jnp.bfloat16)
    grad_out = lax.dot_general(act, grad_b, (((0,), (0,)), ((), ())), preferred_element_type=jnp.float32)
    back = lax.dot_general(grad_b, w_out, (((1,), (1,)), ((), ())), preferred_element_type=jnp.float32)
    _, pull = jax.vjp(jax.nn.gelu, pre)
    grad_pre = pull(back)[0]
    grad_in = lax.dot_general(rows_in, grad_pre.astype(jnp.bfloat16), (((0,), (0,)), ((), ())), preferred_element_type=jnp.float32)
    return (grad_in, lax.optimization_barrier(jnp.sum(grad_pre, axis=0)), grad_out)

def reference(init_field, conduct, nonlin, counts, descriptors, time_code, w_in, bias_in, w_out, decoder):
    inside = jnp.pad(jnp.ones_like(conduct), 1) > 0.5
    cond_pad = jnp.pad(conduct, 1)
    field = init_field
    shots = []
    for step in range(STEPS):
        padded = jnp.pad(field, ((0, 0), (1, 1), (1, 1)))
        field = advance(padded, cond_pad, nonlin, step < counts, inside)
        shots.append(field.astype(jnp.bfloat16))
    snapshots = jnp.stack(shots, axis=1)
    rows_in = (descriptors.astype(jnp.float32)[:, None, :] + time_code.astype(jnp.float32)[None]).astype(jnp.bfloat16).reshape(RUNS * STEPS, P_SIZE)
    pre, act, hidden = trunk(rows_in, w_in, bias_in, w_out)
    cells = GRID_ROWS * GRID_COLS
    weights = decoder.reshape(H, cells)
    scale = 1.0 / (RUNS * STEPS)
    hid_blocks = hidden.reshape(RUNS // 8, 8 * STEPS, H)
    shot_blocks = snapshots.reshape(RUNS // 8, 8 * STEPS, cells)

    def one_block(pair):
        hid, shot = pair
        pred = jnp.dot(hid, weights, preferred_element_type=jnp.float32)
        err = pred - shot.astype(jnp.float32)
        grad_pred = (err * scale).astype(jnp.bfloat16)
        back = lax.dot_general(grad_pred, weights, (((1,), (1,)), ((), ())), preferred_element_type=jnp.float32)
        return (back, jnp.sum(err * err))
    backs, losses = lax.map(one_block, (hid_blocks, shot_blocks))
    dhidden = backs.reshape(RUNS * STEPS, H)
    grad_in, grad_bias, grad_out = trunk_grads(rows_in, pre, act, w_out, dhidden)
    new_w_in = w_in.astype(jnp.float32) - learn_rate * grad_in
    new_bias = bias_in - learn_rate * grad_bias
    new_w_out = w_out.astype(jnp.float32) - learn_rate * grad_out
    mean_loss = jnp.sum(losses) / (RUNS * STEPS * cells)
    return (field, new_w_in, new_bias, new_w_out, mean_loss)
```

```python
import functools

import jax
import jax.numpy as jnp
from jax import lax
from jax.experimental import pallas as pl
from jax.experimental.pallas import tpu as pltpu
from jax.sharding import PartitionSpec as P

time_step = 0.12
learn_rate = 0.5
LANES = 128
SUB = 8
GROUP = 16
f32 = jnp.float32
bf16 = jnp.bfloat16


def neighbours(up, down, axis):
    count = lax.axis_size(axis)
    forward = [(i, i + 1) for i in range(count - 1)]
    backward = [(target, source) for source, target in forward]
    return lax.ppermute(up, axis, forward), lax.ppermute(down, axis, backward)


def kappa_of(u, cond, nonlin):
    divisor = 1.0 + nonlin * u * u
    guess = pl.reciprocal(divisor, approx=True)
    return cond * (guess * (2.0 - divisor * guess))


def pack_kernel(halo, x_ref, top_ref, bottom_ref, low_ref, high_ref):
    per = LANES // halo
    rows_dev, runs, _ = x_ref.shape
    lane = lax.broadcasted_iota(jnp.int32, (runs, LANES), 1)
    for block in range(low_ref.shape[0]):
        low = jnp.zeros((runs, LANES), f32)
        high = jnp.zeros((runs, LANES), f32)
        for place in range(per):
            row = block * per + place
            if row >= rows_dev + 2 * halo:
                break
            if row < halo:
                value = top_ref[row]
            elif row < halo + rows_dev:
                value = x_ref[row - halo]
            else:
                value = bottom_ref[row - halo - rows_dev]
            here = (lane >= place * halo) & (lane < (place + 1) * halo)
            first = pltpu.roll(value, place * halo, 1) if place else value
            shift = (place * halo + halo) % LANES
            last = pltpu.roll(value, shift, 1) if shift else value
            low = jnp.where(here, first, low)
            high = jnp.where(here, last, high)
        low_ref[block] = low
        high_ref[block] = high


def tile_kernel(
    halo, steps, runs, x_ref, top_ref, bottom_ref, left_ref, right_ref, nonlin_ref, counts_ref,
    out_ref, u_ref, c_ref,
):
    rows_dev = x_ref.shape[0]
    rows = rows_dev + 2 * halo
    per = LANES // halo
    lane = lax.broadcasted_iota(jnp.int32, (GROUP, LANES), 1)
    lane_c = lax.broadcasted_iota(jnp.int32, (SUB, LANES), 1)
    row_at, row_count = lax.axis_index("row"), lax.axis_size("row")
    col_at, col_count = lax.axis_index("col"), lax.axis_size("col")

    def padding(row, where, at):
        block, place = row // per, row % per
        left = left_ref[block, where, :]
        right = right_ref[block, where, :]
        shift = LANES - halo - place * halo
        left = pltpu.roll(left, shift, 1) if shift else left
        shift = (LANES - place * halo) % LANES
        right = pltpu.roll(right, shift, 1) if shift else right
        return jnp.where(at < halo, right, jnp.where(at >= LANES - halo, left, 0.0))

    def source(row, where):
        if row < halo:
            return top_ref[row, where, :]
        if row < halo + rows_dev:
            return x_ref[row - halo, where, :]
        return bottom_ref[row - halo - rows_dev, where, :]

    tail = pl.ds(runs, SUB)
    for row in range(rows):
        c_ref[row, :, :LANES] = source(row, tail)
        c_ref[row, :, LANES:] = padding(row, tail, lane_c)

    lane_all = lax.broadcasted_iota(jnp.int32, (GROUP, 2 * LANES), 1)
    inside = (
        (lane_all < LANES)
        | ((lane_all < LANES + halo) & (col_at < col_count - 1))
        | ((lane_all >= 2 * LANES - halo) & (col_at > 0))
    )
    rate = jnp.where(inside, 0.5 * time_step, 0.0)

    def group(index, _):
        where = pl.ds(pl.multiple_of(index * GROUP, GROUP), GROUP)
        for row in range(rows):
            u_ref[row, :, :LANES] = source(row, where)
            u_ref[row, :, LANES:] = padding(row, where, lane)
        nonlin = nonlin_ref[where, :]
        counts = counts_ref[where, :]

        def cond(row):
            return jnp.concatenate([c_ref[row], c_ref[row]], axis=0)

        def step(number, _):
            factor = jnp.where(number < counts, rate, 0.0)

            def one(row, carry, scale):
                u, k, below = carry
                u_next = u_ref[row + 1]
                k_next = kappa_of(u_next, cond(row + 1), nonlin)
                above = (k + k_next) * (u_next - u)
                side = (k + pltpu.roll(k, 2 * LANES - 1, 1)) * (pltpu.roll(u, 2 * LANES - 1, 1) - u)
                flux = (above - below) + (side - pltpu.roll(side, 1, 1))
                u_ref[row] = u + scale * flux
                return u_next, k_next, above

            def several(first, size, scale, unroll, carry):
                def body(i, carry):
                    for inner in range(unroll):
                        carry = one(first + i * unroll + inner, carry, scale)
                    return carry

                return lax.fori_loop(0, size // unroll, body, carry)

            top_scale = jnp.where(row_at > 0, factor, 0.0)
            bottom_scale = jnp.where(row_at < row_count - 1, factor, 0.0)
            u = u_ref[0]
            k = kappa_of(u, cond(0), nonlin)
            u1 = u_ref[1]
            k1 = kappa_of(u1, cond(1), nonlin)
            carry = (u1, k1, (k + k1) * (u1 - u))
            carry = several(1, halo - 1, top_scale, halo - 1, carry)
            carry = several(halo, rows_dev, factor, 4, carry)
            several(halo + rows_dev, halo - 1, bottom_scale, halo - 1, carry)
            return 0

        lax.fori_loop(0, steps, step, 0)
        for row in range(rows_dev):
            out_ref[row, where, :] = u_ref[row + halo, :, :LANES]
        return 0

    lax.fori_loop(0, runs // GROUP, group, 0)


def strip_kernel(
    halo, steps, scale_of, *refs
):
    count = lax.axis_size("col")
    blocks = refs[:count]
    hidden_ref, weights_ref, nonlin_ref, counts_ref, out_ref, loss_ref, u_ref, c_ref, s_ref = refs[count:]
    band, _, wide = s_ref.shape
    rows = band + 2 * halo
    runs = nonlin_ref.shape[0]
    groups = runs // GROUP
    col_at = lax.axis_index("col")
    row_at, row_count = lax.axis_index("row"), lax.axis_size("row")
    has_top = (row_at > 0) | (col_at > 0)
    has_bottom = (row_at < row_count - 1) | (col_at < count - 1)
    lane = lax.broadcasted_iota(jnp.int32, (GROUP, wide), 1)
    first_lane, last_lane = lane == 0, lane == wide - 1

    spots = []
    for back in range(count):
        at = lax.rem(col_at + count - back, count)
        spots.append(pl.ds(pl.multiple_of(at * LANES, LANES), LANES))
    for block, spot in zip(blocks, spots):
        plane = block[rows].astype(f32)
        for row in range(rows):
            c_ref[row, :, spot] = jnp.broadcast_to(plane[row : row + 1], (SUB, LANES))
    loss_ref[...] = jnp.zeros_like(loss_ref)

    def cond(row):
        return jnp.concatenate([c_ref[row], c_ref[row]], axis=0)

    def group(index, _):
        where = pl.ds(pl.multiple_of(index * GROUP, GROUP), GROUP)
        for block, spot in zip(blocks, spots):
            for row in range(rows):
                u_ref[row, :, spot] = block[row, where, :].astype(f32)
        nonlin = nonlin_ref[where, :]
        counts = counts_ref[where, :]

        for number in range(steps):
            factor = jnp.where(number < counts, 0.5 * time_step, 0.0)
            top_scale = jnp.where(has_top, factor, 0.0)
            bottom_scale = jnp.where(has_bottom, factor, 0.0)

            def one(row, carry, scale, keep):
                u, k, below = carry
                u_next = u_ref[row + 1]
                k_next = kappa_of(u_next, cond(row + 1), nonlin)
                above = (k + k_next) * (u_next - u)
                k_right = jnp.where(last_lane, 0.0, pltpu.roll(k, wide - 1, 1))
                u_right = jnp.where(last_lane, 0.0, pltpu.roll(u, wide - 1, 1))
                side = (k + k_right) * (u_right - u)
                before = jnp.where(first_lane, k * u, pltpu.roll(side, 1, 1))
                fresh = u + scale * ((above - below) + (side - before))
                u_ref[row] = fresh
                if keep:
                    s_ref[row - halo, pl.ds(number * GROUP, GROUP), :] = fresh.astype(bf16)
                return u_next, k_next, above

            u = u_ref[number]
            k = kappa_of(u, cond(number), nonlin)
            u1 = u_ref[number + 1]
            k1 = kappa_of(u1, cond(number + 1), nonlin)
            carry = (u1, k1, (k + k1) * (u1 - u))
            for row in range(number + 1, halo):
                carry = one(row, carry, top_scale, False)

            def body(i, carry):
                for inner in range(2):
                    carry = one(halo + i * 2 + inner, carry, factor, True)
                return carry

            carry = lax.fori_loop(0, band // 2, body, carry)
            for row in range(halo + band, rows - 1 - number):
                carry = one(row, carry, bottom_scale, False)

        hidden = hidden_ref[index]

        def learn(row, carry):
            total, loss = carry
            weights = weights_ref[row]
            pred = jnp.dot(hidden, weights, preferred_element_type=f32)
            err = pred - s_ref[row].astype(f32)
            grad = (err * scale_of).astype(bf16)
            total = total + lax.dot_general(
                grad, weights, (((1,), (1,)), ((), ())), preferred_element_type=f32
            )
            return total, loss + jnp.sum(err * err, axis=0, keepdims=True)

        total, loss = lax.fori_loop(
            0,
            band,
            learn,
            (jnp.zeros(out_ref.shape[1:], f32), jnp.zeros((1, wide), f32)),
        )
        out_ref[index] = total.astype(out_ref.dtype)
        loss_ref[...] += loss
        return 0

    lax.fori_loop(0, groups, group, 0)


def per_device(
    init_field, conduct, nonlin, counts, descriptors, time_code, w_in, bias_in, w_out, decoder
):
    runs, rows_dev, cols_dev = init_field.shape
    steps = time_code.shape[0]
    hidden_size = w_out.shape[0]
    run_size = lax.axis_size("run")
    row_size = lax.axis_size("row")
    col_size = lax.axis_size("col")
    halo = steps
    band = rows_dev // col_size
    wide = cols_dev * col_size
    groups = runs // GROUP
    vmem = pltpu.CompilerParams(vmem_limit_bytes=56 * 1024 * 1024)
    any_vmem = pl.BlockSpec(memory_space=pltpu.VMEM)

    tile = jnp.concatenate(
        [
            jnp.swapaxes(init_field, 0, 1),
            jnp.broadcast_to(conduct[:, None, :], (rows_dev, SUB, cols_dev)),
        ],
        axis=1,
    )
    top, bottom = neighbours(tile[rows_dev - halo :], tile[:halo], "row")

    padded = jnp.concatenate([top, tile, bottom], axis=0).astype(bf16)
    col_at = lax.axis_index("col")

    def message(target):
        part = lax.dynamic_slice_in_dim(padded, target * band, band + 2 * halo, 0)
        plane = jnp.pad(part[:, runs], ((0, runs - band - 2 * halo), (0, 0)))
        return jnp.concatenate([part[:, :runs], plane[None]], axis=0)

    blocks = [message(col_at)]
    for hop in range(1, col_size):
        pairs = [(i, (i + hop) % col_size) for i in range(col_size)]
        blocks.append(lax.ppermute(message((col_at + hop) % col_size), "col", pairs))

    packs = -(-(rows_dev + 2 * halo) // (LANES // halo))
    pack_shape = jax.ShapeDtypeStruct((packs, runs + SUB, LANES), f32)
    low, high = pl.pallas_call(
        functools.partial(pack_kernel, halo),
        out_shape=(pack_shape, pack_shape),
        in_specs=[any_vmem] * 3,
        out_specs=(any_vmem, any_vmem),
        compiler_params=vmem,
        name="pack_columns",
    )(tile, top, bottom)
    left, right = neighbours(high, low, "col")

    field = pl.pallas_call(
        functools.partial(tile_kernel, halo, steps, runs),
        out_shape=jax.ShapeDtypeStruct((rows_dev, runs, cols_dev), f32),
        in_specs=[any_vmem] * 7,
        out_specs=any_vmem,
        scratch_shapes=[
            pltpu.VMEM((rows_dev + 2 * halo, GROUP, 2 * LANES), f32),
            pltpu.VMEM((rows_dev + 2 * halo, SUB, 2 * LANES), f32),
        ],
        compiler_params=vmem,
        cost_estimate=pl.CostEstimate(flops=10**8, bytes_accessed=10**7, transcendentals=0),
        name="tile_solver",
    )(
        tile,
        top,
        bottom,
        left,
        right,
        jnp.broadcast_to(nonlin[:, None], (runs, 2 * LANES)),
        jnp.broadcast_to(counts[:, None], (runs, 2 * LANES)),
    )
    final_field = jnp.swapaxes(field, 0, 1)

    runs_total = runs * run_size
    rows_all = runs_total * steps
    desc = descriptors.astype(f32).reshape(run_size * groups, 1, GROUP, -1)
    codes = time_code.astype(f32)[None, :, None, :]
    rows_in = (desc + codes).astype(bf16).reshape(rows_all, -1)
    pre = jnp.dot(rows_in, w_in, preferred_element_type=f32) + bias_in
    act = jax.nn.gelu(pre).astype(bf16)
    hidden = jnp.dot(act, w_out, preferred_element_type=f32).astype(bf16)
    mine = lax.dynamic_slice_in_dim(
        hidden.reshape(run_size, groups, GROUP * steps, hidden_size), lax.axis_index("run"), 1, 0
    )[0]
    weights = jnp.swapaxes(decoder, 0, 1)

    partial, loss = pl.pallas_call(
        functools.partial(strip_kernel, halo, steps, 1.0 / rows_all),
        out_shape=(
            jax.ShapeDtypeStruct((groups, GROUP * steps, hidden_size), bf16),
            jax.ShapeDtypeStruct((1, wide), f32),
        ),
        in_specs=[any_vmem] * (col_size + 4),
        out_specs=(any_vmem, any_vmem),
        scratch_shapes=[
            pltpu.VMEM((band + 2 * halo, GROUP, wide), f32),
            pltpu.VMEM((band + 2 * halo, SUB, wide), f32),
            pltpu.VMEM((band, GROUP * steps, wide), bf16),
        ],
        compiler_params=vmem,
        cost_estimate=pl.CostEstimate(flops=10**8, bytes_accessed=10**7, transcendentals=0),
        name="strip_solver",
    )(
        *blocks,
        mine,
        weights,
        jnp.broadcast_to(nonlin[:, None], (runs, wide)),
        jnp.broadcast_to(counts[:, None], (runs, wide)),
    )

    cells = row_size * col_size
    share = runs * steps // cells
    pieces = lax.all_to_all(
        partial.reshape(cells, share, hidden_size), ("row", "col"), 0, 0, tiled=True
    )
    summed = jnp.sum(pieces.astype(f32), axis=0).astype(bf16)
    gathered = lax.all_to_all(
        jnp.broadcast_to(summed[None], (cells, share, hidden_size)),
        ("row", "col"),
        0,
        0,
        tiled=True,
    ).reshape(runs * steps, hidden_size)
    swap = [(i, (i + 1) % run_size) for i in range(run_size)]
    other = lax.ppermute(gathered, "run", swap)
    first = lax.axis_index("run") == 0
    grad_b = jnp.concatenate(
        [jnp.where(first, gathered, other), jnp.where(first, other, gathered)], axis=0
    )
    loss_total = lax.psum(jnp.sum(loss), ("run", "row", "col"))

    grad_out = lax.dot_general(act, grad_b, (((0,), (0,)), ((), ())), preferred_element_type=f32)
    back = lax.dot_general(grad_b, w_out, (((1,), (1,)), ((), ())), preferred_element_type=f32)
    _, pull = jax.vjp(jax.nn.gelu, pre)
    grad_pre = pull(back)[0]
    grad_in = lax.dot_general(
        rows_in, grad_pre.astype(bf16), (((0,), (0,)), ((), ())), preferred_element_type=f32
    )
    new_w_in = w_in.astype(f32) - learn_rate * grad_in
    new_bias = bias_in - learn_rate * jnp.sum(grad_pre, axis=0)
    new_w_out = w_out.astype(f32) - learn_rate * grad_out
    mean_loss = loss_total / (rows_all * rows_dev * row_size * wide)
    return (final_field, new_w_in, new_bias, new_w_out, mean_loss)


def solution(mesh):
    in_specs = (
        P("run", "row", "col"),
        P("row", "col"),
        P("run"),
        P("run"),
        P(),
        P(),
        P(),
        P(),
        P(),
        P(None, ("row", "col"), None),
    )
    out_specs = (P("run", "row", "col"), P(), P(), P(), P())
    return jax.shard_map(
        per_device, mesh=mesh, in_specs=in_specs, out_specs=out_specs, check_vma=False
    )
```

```python
import functools

import jax
import jax.numpy as jnp
import numpy as np
from jax import lax
from jax.experimental import pallas as pl
from jax.experimental.pallas import tpu as pltpu
from jax.sharding import PartitionSpec as P

time_step = 0.12
learn_rate = 0.5
LANES = 128
SUB = 8
GROUP = 16
f32 = jnp.float32
bf16 = jnp.bfloat16


def neighbours(up, down, axis):
    count = lax.axis_size(axis)
    forward = [(i, i + 1) for i in range(count - 1)]
    backward = [(target, source) for source, target in forward]
    return lax.ppermute(up, axis, forward), lax.ppermute(down, axis, backward)


def kappa_of(u, cond, nonlin):
    divisor = 1.0 + nonlin * (u * u)
    guess = pltpu.reciprocal(divisor, approx=True)
    return cond * (guess * (2.0 - divisor * guess))


def apart(wide):
    parts = wide // LANES
    source = np.arange(wide)[:, None]
    place = np.arange(wide)[None, :]
    return jnp.asarray(source == parts * (place % LANES) + place // LANES, bf16)


def decoder_kernel(d_ref, order_ref, out_ref, wide_ref):
    size, band, wide = d_ref.shape
    x = d_ref[...]
    if band % 16:
        x = x.astype(f32).reshape(size * band, wide).astype(bf16)
    else:
        x = x.reshape(size * band, wide)
    y = jnp.dot(x, order_ref[...], preferred_element_type=f32)
    for part in range(wide // LANES):
        wide_ref[part] = y[:, part * LANES : (part + 1) * LANES]
    for row in range(band):
        for part in range(wide // LANES):
            lanes = pl.ds(row * wide + part * LANES, LANES)
            out_ref[:, lanes] = wide_ref[part, pl.ds(row, size, stride=band), :].astype(bf16)


ROW_SEGS = 8
COL_SEGS = 16


def tile_order(halo, cols_dev):
    across = (cols_dev + 2 * halo) // COL_SEGS
    lanes = ROW_SEGS * COL_SEGS
    place = np.arange(across * lanes)
    column = (place % COL_SEGS) * across + place // lanes
    seg_row = (place % lanes) // COL_SEGS
    source = np.arange(ROW_SEGS * cols_dev)[:, None]
    main = (source // cols_dev == seg_row) & (source % cols_dev + halo == column)
    half = ROW_SEGS * halo
    parity = np.arange(2)[:, None, None, None]
    high = np.arange(2)[:, None, None]
    source = np.arange(LANES)[:, None]
    edge = (
        (source // half == parity)
        & (source % half // halo == seg_row)
        & (source % halo + high * (cols_dev + halo) == column)
    )
    return jnp.asarray(main, bf16), jnp.asarray(edge.reshape(2, 2 * LANES, -1), bf16)


def row_source(halo, rows_dev, runs, refs):
    x_ref, cond_ref, top_ref, bottom_ref = refs

    def source(row):
        if row < halo:
            return top_ref[pl.ds(row, runs, stride=halo), :], top_ref[pl.ds(runs * halo + row, 1), :]
        row -= halo
        if row < rows_dev:
            return x_ref[pl.ds(row, runs, stride=rows_dev), :], cond_ref[pl.ds(row, 1), :]
        row -= rows_dev
        return (
            bottom_ref[pl.ds(row, runs, stride=halo), :],
            bottom_ref[pl.ds(runs * halo + row, 1), :],
        )

    def both(row, copies):
        runs_of, cond = source(row)
        return jnp.concatenate([runs_of, jnp.broadcast_to(cond, (copies, LANES))], axis=0)

    return both


def pack_kernel(halo, runs, x_ref, cond_ref, top_ref, bottom_ref, low_ref, high_ref):
    rows_dev = cond_ref.shape[0]
    source = row_source(halo, rows_dev, runs, (x_ref, cond_ref, top_ref, bottom_ref))
    deep = (rows_dev + 2 * halo) // ROW_SEGS
    half = ROW_SEGS * halo
    lane = lax.broadcasted_iota(jnp.int32, (runs + SUB, LANES), 1)
    for block in range(low_ref.shape[0]):
        low = jnp.zeros((runs + SUB, LANES), f32)
        high = jnp.zeros((runs + SUB, LANES), f32)
        for parity in range(2):
            if 2 * block + parity >= deep:
                break
            for seg in range(ROW_SEGS):
                value = source(seg * deep + 2 * block + parity, SUB)
                spot = parity * half + seg * halo
                here = (lane >= spot) & (lane < spot + halo)
                first = pltpu.roll(value, spot, 1) if spot else value
                shift = (spot + halo) % LANES
                last = pltpu.roll(value, shift, 1) if shift else value
                low = jnp.where(here, first, low)
                high = jnp.where(here, last, high)
        low_ref[block] = low
        high_ref[block] = high


PIECES = 3


def pieces_of(x):
    high = x.astype(bf16)
    rest = x - high.astype(f32)
    middle = rest.astype(bf16)
    return high, middle, (rest - middle.astype(f32)).astype(bf16)


def tile_kernel(
    halo, steps, runs, x_ref, cond_ref, top_ref, bottom_ref, left_ref, right_ref, nonlin_ref,
    counts_ref, main_ref, edge_ref, out_ref, u_ref, c_ref, rate_ref, body_ref, ends_ref, back_ref,
):
    rows_dev, cols_dev = cond_ref.shape
    source = row_source(halo, rows_dev, runs, (x_ref, cond_ref, top_ref, bottom_ref))
    deep = (rows_dev + 2 * halo) // ROW_SEGS
    across = (cols_dev + 2 * halo) // COL_SEGS
    tall = runs + GROUP
    row_at, row_count = lax.axis_index("row"), lax.axis_size("row")
    col_at, col_count = lax.axis_index("col"), lax.axis_size("col")

    for b in range(deep):
        for seg in range(ROW_SEGS):
            for i, piece in enumerate(pieces_of(source(seg * deep + b, GROUP))):
                body_ref[i, b * tall : (b + 1) * tall, seg * cols_dev : (seg + 1) * cols_dev] = piece
        for side, ref in enumerate((left_ref, right_ref)):
            value = jnp.concatenate([ref[b // 2], ref[b // 2, runs:]], axis=0)
            for i, piece in enumerate(pieces_of(value)):
                first = b // 2 * tall
                ends_ref[i, b % 2, first : first + tall, side * LANES : (side + 1) * LANES] = piece

    lane = lax.broadcasted_iota(jnp.int32, (SUB, LANES), 1)
    chunk = 3 if across % 3 == 0 else 1
    for start in range(0, across, chunk):
        lanes = slice(start * LANES, (start + chunk) * LANES)
        total = None
        for i in range(PIECES):
            part = jnp.dot(body_ref[i], main_ref[:, lanes], preferred_element_type=f32)
            total = part if total is None else total + part
        extra = []
        for parity in range(2):
            more = None
            for i in range(PIECES):
                part = jnp.dot(
                    ends_ref[i, parity], edge_ref[parity, :, lanes], preferred_element_type=f32
                )
                more = part if more is None else more + part
            extra.append(more)
        for b in range(deep):
            first = b // 2 * tall
            value = total[b * tall : (b + 1) * tall] + extra[b % 2][first : first + tall]
            for inner in range(chunk):
                q = start + inner
                here = value[:, inner * LANES : (inner + 1) * LANES]
                u_ref[0, b, q] = here[:runs]
                c_ref[b + 1, q] = here[runs : runs + SUB]
    for b in range(deep):
        for q in range(across):
            row = lane // COL_SEGS * deep + b
            col = lane % COL_SEGS * across + q
            inside = (
                ((row >= halo) | (row_at > 0))
                & ((row < halo + rows_dev) | (row_at < row_count - 1))
                & ((col >= halo) | (col_at > 0))
                & ((col < halo + cols_dev) | (col_at < col_count - 1))
            )
            rate_ref[b, q] = jnp.where(inside, 0.5 * time_step, 0.0)
    for q in range(across):
        c_ref[0, q] = pltpu.roll(c_ref[deep, q], COL_SEGS, 1)
        c_ref[deep + 1, q] = pltpu.roll(c_ref[1, q], LANES - COL_SEGS, 1)

    def group(index, _):
        where = pl.ds(pl.multiple_of(index * SUB, SUB), SUB)
        nonlin = nonlin_ref[where, :]
        counts = counts_ref[where, :]

        def step(number, old, new):
            active = jnp.where(number < counts, 1.0, 0.0)

            def get(b, q):
                if b < 0:
                    u = pltpu.roll(u_ref[old, deep - 1, q, where, :], COL_SEGS, 1)
                elif b == deep:
                    u = pltpu.roll(u_ref[old, 0, q, where, :], LANES - COL_SEGS, 1)
                else:
                    u = u_ref[old, b, q, where, :]
                return u, kappa_of(u, c_ref[b + 1, q], nonlin)

            last = [get(-1, q) for q in range(across)]
            here = [get(0, q) for q in range(across)]
            below = [(k0 + k1) * (u1 - u0) for (u0, k0), (u1, k1) in zip(last, here)]
            for b in range(deep):
                u = [pair[0] for pair in here]
                k = [pair[1] for pair in here]
                u.append(pltpu.roll(u[0], LANES - 1, 1))
                k.append(pltpu.roll(k[0], LANES - 1, 1))
                side = [(k[q] + k[q + 1]) * (u[q + 1] - u[q]) for q in range(across)]
                side.append(pltpu.roll(side[across - 1], 1, 1))
                then = [get(b + 1, q) for q in range(across)]
                above = [(k[q] + then[q][1]) * (then[q][0] - u[q]) for q in range(across)]
                for q in range(across):
                    flux = (above[q] - below[q]) + (side[q] - side[q - 1])
                    u_ref[new, b, q, where, :] = u[q] + (rate_ref[b, q] * active) * flux
                here, below = then, above

        def two(i, _):
            step(2 * i, 0, 1)
            step(2 * i + 1, 1, 0)
            return 0

        lax.fori_loop(0, steps // 2, two, 0)
        return 0

    lax.fori_loop(0, runs // SUB, group, 0)

    for b in range(deep):
        for q in range(across):
            for i, piece in enumerate(pieces_of(u_ref[0, b, q])):
                back_ref[i, b * runs : (b + 1) * runs, q * LANES : (q + 1) * LANES] = piece
    chunk = 2 if ROW_SEGS % 2 == 0 else 1
    for start in range(0, ROW_SEGS, chunk):
        places = slice(start * cols_dev, (start + chunk) * cols_dev)
        total = None
        for i in range(PIECES):
            part = lax.dot_general(
                back_ref[i], main_ref[places, :], (((1,), (1,)), ((), ())), preferred_element_type=f32
            )
            total = part if total is None else total + part
        for b in range(deep):
            for inner in range(chunk):
                row = (start + inner) * deep + b - halo
                if 0 <= row < rows_dev:
                    out_ref[pl.ds(row, runs, stride=rows_dev), :] = total[
                        b * runs : (b + 1) * runs, inner * cols_dev : (inner + 1) * cols_dev
                    ]


def strip_kernel(halo, steps, runs, *refs):
    count = lax.axis_size("col")
    blocks = refs[:count]
    order_ref, nonlin_ref, counts_ref = refs[count : count + 3]
    out_ref, square_ref, u_ref, c_ref, turned_ref, wide_ref = refs[count + 4 :]
    cols_dev = blocks[0].shape[2]
    wide = count * cols_dev
    parts = wide // LANES
    rows = u_ref.shape[0]
    band = rows - 2 * halo
    index = pl.program_id(0)
    col_at = lax.axis_index("col")
    row_at, row_count = lax.axis_index("row"), lax.axis_size("row")
    has_top = (row_at > 0) | (col_at > 0)
    has_bottom = (row_at < row_count - 1) | (col_at < count - 1)
    lane = lax.broadcasted_iota(jnp.int32, (GROUP, LANES), 1)
    first_lane, last_lane = lane == 0, lane == LANES - 1

    def ordered(get):
        whole = jnp.concatenate([get(block) for block in blocks], axis=1)
        return jnp.dot(whole, turned_ref[...], preferred_element_type=f32)

    @pl.when(index == 0)
    def _():
        for back in range(count):
            at = lax.rem(col_at + count - back, count)
            turned_ref[back * cols_dev : (back + 1) * cols_dev, :] = order_ref[
                pl.ds(pl.multiple_of(at * cols_dev, cols_dev), cols_dev), :
            ]
        plane = ordered(lambda block: block[runs])
        for row in range(rows):
            c_ref[row] = jnp.broadcast_to(plane[row : row + 1], (SUB, wide))
        square_ref[...] = jnp.zeros_like(square_ref)

    def split(x):
        return [x[..., part * LANES : (part + 1) * LANES] for part in range(parts)]

    where = pl.ds(pl.multiple_of(index * GROUP, GROUP), GROUP)
    fields = ordered(lambda block: block[where].reshape(GROUP * rows, cols_dev))
    for part, values in enumerate(split(fields)):
        wide_ref[part] = values
    for row in range(rows):
        for part in range(parts):
            lanes = pl.ds(part * LANES, LANES)
            u_ref[row, :, lanes] = wide_ref[part, pl.ds(row, GROUP, stride=rows), :]
    nonlin = nonlin_ref[where, :]
    counts = counts_ref[where, :]

    def get(row):
        u = split(u_ref[row])
        cond = split(jnp.concatenate([c_ref[row]] * (GROUP // SUB), axis=0))
        return u, [kappa_of(a, b, nonlin) for a, b in zip(u, cond)]

    for number in range(steps):
        factor = jnp.where(number < counts, 0.5 * time_step, 0.0)
        top_scale = jnp.where(has_top, factor, 0.0)
        bottom_scale = jnp.where(has_bottom, factor, 0.0)

        def one(row, carry, scale, keep):
            u, k, below, square = carry
            then_u, then_k = get(row + 1)
            above = [(a + b) * (c - d) for a, b, c, d in zip(k, then_k, then_u, u)]
            u_more = u + [jnp.where(last_lane, 0.0, pltpu.roll(u[0], LANES - 1, 1))]
            k_more = k + [jnp.where(last_lane, 0.0, pltpu.roll(k[0], LANES - 1, 1))]
            side = [(k_more[p] + k_more[p + 1]) * (u_more[p + 1] - u_more[p]) for p in range(parts)]
            start = jnp.where(first_lane, k[0] * u[0], pltpu.roll(side[-1], 1, 1))
            side = [start] + side
            for p in range(parts):
                fresh = u[p] + scale * ((above[p] - below[p]) + (side[p + 1] - side[p]))
                u_ref[row, :, pl.ds(p * LANES, LANES)] = fresh
                if keep:
                    shot = fresh.astype(bf16)
                    lanes = pl.ds((row - halo) * wide + p * LANES, LANES)
                    out_ref[0, pl.ds(number * GROUP, GROUP), lanes] = shot
                    again = shot.astype(f32)
                    square = square + again * again
            return then_u, then_k, above, square

        last_u, last_k = get(number)
        u, k = get(number + 1)
        below = [(a + b) * (c - d) for a, b, c, d in zip(k, last_k, u, last_u)]
        carry = (u, k, below, jnp.zeros((GROUP, LANES), f32))
        for row in range(number + 1, halo):
            carry = one(row, carry, top_scale, False)
        for row in range(halo, halo + band):
            carry = one(row, carry, factor, True)
        for row in range(halo + band, rows - 1 - number):
            carry = one(row, carry, bottom_scale, False)
        square_ref[...] += carry[3]


def share_kernel(scale_of, pieces_ref, loss_ref, out_ref):
    total = pieces_ref[0].astype(f32)
    for source in range(1, pieces_ref.shape[0]):
        total = total + pieces_ref[source].astype(f32)
    rows = [piece.astype(f32) for piece in pieces_of(loss_ref[...])]
    filler = jnp.zeros((out_ref.shape[1] - total.shape[0] - PIECES, total.shape[1]), f32)
    message = jnp.concatenate([total] + rows + [filler], axis=0).astype(bf16)
    for target in range(out_ref.shape[0]):
        out_ref[target] = message


def finish_kernel(
    share, loss_scale, mine_ref, other_ref, act_ref, slope_ref, rows_ref, w_in_ref, bias_ref,
    w_out_ref, new_in_ref, new_bias_ref, new_out_ref, loss_ref, grad_ref, parts_ref,
):
    core = lax.axis_index("run")
    cells = mine_ref.shape[0]
    for at, ref in ((core, mine_ref), (1 - core, other_ref)):
        parts = jnp.zeros((1, ref.shape[2]), f32)
        rows = []
        for source in range(cells):
            value = ref[source].astype(f32)
            rows.append(value[:share])
            for piece in range(PIECES):
                parts = parts + value[share + piece : share + piece + 1]
        size = cells * share
        grad_ref[pl.ds(pl.multiple_of(at * size, size), size), :] = jnp.concatenate(
            rows, axis=0
        ).astype(bf16)
        parts_ref[pl.ds(at, 1), :] = parts
    loss = jnp.sum(parts_ref[0:1] + parts_ref[1:2], axis=1, keepdims=True) * loss_scale
    loss_ref[...] = jnp.broadcast_to(loss, loss_ref.shape)
    grad = grad_ref[...]
    by_rows = (((0,), (0,)), ((), ()))
    grad_out = lax.dot_general(act_ref[...], grad, by_rows, preferred_element_type=f32)
    new_out_ref[...] = w_out_ref[...].astype(f32) - learn_rate * grad_out
    back = lax.dot_general(
        grad, w_out_ref[...], (((1,), (1,)), ((), ())), preferred_element_type=f32
    )
    grad_pre = back * slope_ref[...]
    new_bias_ref[...] = bias_ref[...] - learn_rate * jnp.sum(grad_pre, axis=0, keepdims=True)
    grad_in = lax.dot_general(
        rows_ref[...], grad_pre.astype(bf16), by_rows, preferred_element_type=f32
    )
    new_in_ref[...] = w_in_ref[...].astype(f32) - learn_rate * grad_in


def per_device(
    init_field, conduct, nonlin, counts, descriptors, time_code, w_in, bias_in, w_out, decoder
):
    runs, rows_dev, cols_dev = init_field.shape
    steps = time_code.shape[0]
    inputs, hidden_size = w_in.shape
    run_size = lax.axis_size("run")
    row_size = lax.axis_size("row")
    col_size = lax.axis_size("col")
    halo = steps
    band = rows_dev // col_size
    rows_strip = band + 2 * halo
    wide = cols_dev * col_size
    groups = runs // GROUP
    runs_total = runs * run_size
    rows_all = runs_total * steps
    scale_of = 1.0 / rows_all
    vmem = pltpu.CompilerParams(vmem_limit_bytes=56 * 1024 * 1024)
    in_vmem = pl.BlockSpec(memory_space=pltpu.VMEM)
    anywhere = pl.BlockSpec(memory_space=pl.ANY)

    tile = jnp.concatenate([init_field, conduct[None]], axis=0)
    top, bottom = neighbours(tile[:, rows_dev - halo :], tile[:, :halo], "row")

    padded = jnp.concatenate([top, tile, bottom], axis=1).astype(bf16)
    col_at = lax.axis_index("col")

    def message(target):
        return lax.dynamic_slice_in_dim(padded, target * band, rows_strip, 1)

    messages = [message((col_at + hop) % col_size) for hop in range(col_size)]

    deep = (rows_dev + 2 * halo) // ROW_SEGS
    across = (cols_dev + 2 * halo) // COL_SEGS
    tall = runs + GROUP
    tile_args = (
        init_field.reshape(runs * rows_dev, cols_dev),
        conduct,
        top.reshape(-1, cols_dev),
        bottom.reshape(-1, cols_dev),
    )
    pack_shape = jax.ShapeDtypeStruct((-(-deep // 2), runs + SUB, LANES), f32)
    low, high = pl.pallas_call(
        functools.partial(pack_kernel, halo, runs),
        out_shape=(pack_shape, pack_shape),
        in_specs=[in_vmem] * 4,
        out_specs=(in_vmem, in_vmem),
        compiler_params=vmem,
        name="pack_columns",
    )(*tile_args)
    (low, high, decoder), messages = lax.optimization_barrier(((low, high, decoder), messages))
    left, right = neighbours(high, low, "col")
    blocks = messages[:1]
    for hop in range(1, col_size):
        pairs = [(i, (i + hop) % col_size) for i in range(col_size)]
        blocks.append(lax.ppermute(messages[hop], "col", pairs))

    nonlin_wide = jnp.broadcast_to(nonlin[:, None], (runs, LANES))
    counts_wide = jnp.broadcast_to(counts[:, None], (runs, LANES))
    field = pl.pallas_call(
        functools.partial(tile_kernel, halo, steps, runs),
        out_shape=jax.ShapeDtypeStruct((runs * rows_dev, cols_dev), f32),
        in_specs=[in_vmem] * 10,
        out_specs=in_vmem,
        scratch_shapes=[
            pltpu.VMEM((2, deep, across, runs, LANES), f32),
            pltpu.VMEM((deep + 2, across, SUB, LANES), f32),
            pltpu.VMEM((deep, across, SUB, LANES), f32),
            pltpu.VMEM((PIECES, deep * tall, ROW_SEGS * cols_dev), bf16),
            pltpu.VMEM((PIECES, 2, -(-deep // 2) * tall, 2 * LANES), bf16),
            pltpu.VMEM((PIECES, deep * runs, across * LANES), bf16),
        ],
        compiler_params=vmem,
        name="tile_solver",
    )(*tile_args, left, right, nonlin_wide, counts_wide, *tile_order(halo, cols_dev))
    final_field = field.reshape(init_field.shape)

    desc = descriptors.astype(f32).reshape(run_size * groups, 1, GROUP, -1)
    codes = time_code.astype(f32)[None, :, None, :]
    rows_in = (desc + codes).astype(bf16).reshape(rows_all, -1)
    pre = jnp.dot(rows_in, w_in, preferred_element_type=f32) + bias_in
    act, pull = jax.vjp(jax.nn.gelu, pre)
    slope = pull(jnp.ones_like(pre))[0]
    act = act.astype(bf16)
    hidden = jnp.dot(act, w_out, preferred_element_type=f32).astype(bf16)
    hidden, slope = lax.optimization_barrier((hidden, slope))
    mine = lax.dynamic_slice_in_dim(hidden, lax.axis_index("run") * runs * steps, runs * steps, 0)

    order = apart(wide)
    size = 64
    weights = pl.pallas_call(
        decoder_kernel,
        grid=(hidden_size // size,),
        out_shape=jax.ShapeDtypeStruct((hidden_size, band * wide), bf16),
        in_specs=[
            pl.BlockSpec((size, band, wide), lambda i: (i, 0, 0)),
            pl.BlockSpec((wide, wide), lambda i: (0, 0)),
        ],
        out_specs=pl.BlockSpec((size, band * wide), lambda i: (i, 0)),
        scratch_shapes=[pltpu.VMEM((wide // LANES, size * band, LANES), f32)],
        compiler_params=vmem,
        name="decoder_order",
    )(decoder, order)
    last_dims = (((1,), (1,)), ((), ()))
    gram = lax.dot_general(weights, weights, last_dims, preferred_element_type=f32)
    pushed = None
    rest = gram
    for _ in range(PIECES):
        piece = lax.reduce_precision(rest, 8, 7)
        rest = rest - piece
        part = jnp.dot(mine, piece.astype(bf16), preferred_element_type=f32)
        pushed = part if pushed is None else pushed + part

    shots, squares = pl.pallas_call(
        functools.partial(strip_kernel, halo, steps, runs),
        grid=(groups,),
        out_shape=(
            jax.ShapeDtypeStruct((groups, GROUP * steps, band * wide), bf16),
            jax.ShapeDtypeStruct((GROUP, LANES), f32),
        ),
        in_specs=[in_vmem] * (col_size + 3) + [anywhere],
        out_specs=(
            pl.BlockSpec((1, GROUP * steps, band * wide), lambda i: (i, 0, 0)),
            pl.BlockSpec((GROUP, LANES), lambda i: (0, 0)),
        ),
        scratch_shapes=[
            pltpu.VMEM((rows_strip, GROUP, wide), f32),
            pltpu.VMEM((rows_strip, SUB, wide), f32),
            pltpu.VMEM((wide, wide), bf16),
            pltpu.VMEM((wide // LANES, GROUP * rows_strip, LANES), f32),
        ],
        compiler_params=vmem,
        name="strip_solver",
    )(*blocks, order, nonlin_wide, counts_wide, field)

    drawn = lax.dot_general(
        shots.reshape(runs * steps, band * wide), weights, last_dims, preferred_element_type=f32
    )
    partial = ((pushed - drawn) * scale_of).astype(bf16)
    loss = jnp.sum(mine.astype(f32) * (pushed - 2.0 * drawn), axis=0, keepdims=True)
    loss = loss + jnp.pad(jnp.sum(squares, axis=0, keepdims=True), ((0, 0), (0, hidden_size - LANES)))

    cells = row_size * col_size
    share = runs * steps // cells
    pieces = lax.all_to_all(
        partial.reshape(cells, share, hidden_size), ("row", "col"), 0, 0, tiled=True
    )
    taller = -(-(share + PIECES) // 16) * 16
    message_out = pl.pallas_call(
        functools.partial(share_kernel, scale_of),
        out_shape=jax.ShapeDtypeStruct((cells, taller, hidden_size), bf16),
        in_specs=[in_vmem] * 2,
        out_specs=in_vmem,
        compiler_params=vmem,
        name="share_sum",
    )(pieces, loss)
    gathered = lax.all_to_all(message_out, ("row", "col"), 0, 0, tiled=True)
    swap = [(i, (i + 1) % run_size) for i in range(run_size)]
    other = lax.ppermute(gathered, "run", swap)
    cells_total = rows_dev * row_size * wide
    new_w_in, new_bias, new_w_out, mean_loss = pl.pallas_call(
        functools.partial(finish_kernel, share, 1.0 / (rows_all * cells_total)),
        out_shape=(
            jax.ShapeDtypeStruct((inputs, hidden_size), f32),
            jax.ShapeDtypeStruct((1, hidden_size), f32),
            jax.ShapeDtypeStruct((hidden_size, hidden_size), f32),
            jax.ShapeDtypeStruct((1, LANES), f32),
        ),
        in_specs=[in_vmem] * 8,
        out_specs=(in_vmem,) * 4,
        scratch_shapes=[
            pltpu.VMEM((rows_all, hidden_size), bf16),
            pltpu.VMEM((run_size, hidden_size), f32),
        ],
        compiler_params=vmem,
        name="trunk_update",
    )(gathered, other, act, slope, rows_in, w_in, bias_in[None], w_out)
    return (final_field, new_w_in, new_bias[0], new_w_out, mean_loss[0, 0])


def solution(mesh):
    in_specs = (
        P("run", "row", "col"),
        P("row", "col"),
        P("run"),
        P("run"),
        P(),
        P(),
        P(),
        P(),
        P(),
        P(None, ("row", "col"), None),
    )
    out_specs = (P("run", "row", "col"), P(), P(), P(), P())
    return jax.shard_map(
        per_device, mesh=mesh, in_specs=in_specs, out_specs=out_specs, check_vma=False
    )
```

```python
import functools

import jax
import jax.numpy as jnp
import numpy as np
from jax import lax
from jax.experimental import pallas as pl
from jax.experimental.pallas import tpu as pltpu
from jax.sharding import PartitionSpec as P

time_step = 0.12
learn_rate = 0.5
LANES = 128
SUB = 8
GROUP = 16
f32 = jnp.float32
bf16 = jnp.bfloat16


def neighbours(up, down, axis):
    count = lax.axis_size(axis)
    forward = [(i, i + 1) for i in range(count - 1)]
    backward = [(target, source) for source, target in forward]
    return lax.ppermute(up, axis, forward), lax.ppermute(down, axis, backward)


def kappa_of(u, cond, inverse):
    return cond * pltpu.reciprocal(inverse + u * u, approx=True)


def apart(wide):
    parts = wide // LANES
    source = np.arange(wide)[:, None]
    place = np.arange(wide)[None, :]
    return jnp.asarray(source == parts * (place % LANES) + place // LANES, bf16)


def reorder(index, size, d_ref, order_ref, out_ref, wide_ref):
    _, band, wide = d_ref.shape
    here = pl.ds(pl.multiple_of(index * size, size), size)
    x = d_ref[here]
    if band % 16:
        x = x.astype(f32).reshape(size * band, wide).astype(bf16)
    else:
        x = x.reshape(size * band, wide)
    y = jnp.dot(x, order_ref[...], preferred_element_type=f32)
    for part in range(wide // LANES):
        wide_ref[part] = y[:, part * LANES : (part + 1) * LANES]
    for row in range(band):
        for part in range(wide // LANES):
            lanes = pl.ds(row * wide + part * LANES, LANES)
            out_ref[here, lanes] = wide_ref[part, pl.ds(row, size, stride=band), :].astype(bf16)


def product(left_ref, right_ref):
    cells = left_ref.shape[1]
    size = min(cells, 2048)
    total = None
    for start in range(0, cells, size):
        part = lax.dot_general(
            left_ref[:, start : start + size],
            right_ref[:, start : start + size],
            (((1,), (1,)), ((), ())),
            preferred_element_type=f32,
        )
        total = part if total is None else total + part
    return total


ROW_SEGS = 8
COL_SEGS = 16


def tile_order(halo, cols_dev):
    across = (cols_dev + 2 * halo) // COL_SEGS
    lanes = ROW_SEGS * COL_SEGS
    place = np.arange(across * lanes)
    column = (place % COL_SEGS) * across + place // lanes
    seg_row = (place % lanes) // COL_SEGS
    source = np.arange(ROW_SEGS * cols_dev)[:, None]
    main = (source // cols_dev == seg_row) & (source % cols_dev + halo == column)
    half = ROW_SEGS * halo
    parity = np.arange(2)[:, None, None, None]
    high = np.arange(2)[:, None, None]
    source = np.arange(LANES)[:, None]
    edge = (
        (source // half == parity)
        & (source % half // halo == seg_row)
        & (source % halo + high * (cols_dev + halo) == column)
    )
    return jnp.asarray(main, bf16), jnp.asarray(edge.reshape(2, 2 * LANES, -1), bf16)


def row_source(halo, rows_dev, runs, refs):
    x_ref, cond_ref, top_ref, bottom_ref = refs

    def source(row):
        if row < halo:
            return top_ref[pl.ds(row, runs, stride=halo), :], top_ref[pl.ds(runs * halo + row, 1), :]
        row -= halo
        if row < rows_dev:
            return x_ref[pl.ds(row, runs, stride=rows_dev), :], cond_ref[pl.ds(row, 1), :]
        row -= rows_dev
        return (
            bottom_ref[pl.ds(row, runs, stride=halo), :],
            bottom_ref[pl.ds(runs * halo + row, 1), :],
        )

    def both(row, copies):
        runs_of, cond = source(row)
        return jnp.concatenate([runs_of, jnp.broadcast_to(cond, (copies, LANES))], axis=0)

    return both


def pack_kernel(halo, runs, x_ref, cond_ref, top_ref, bottom_ref, low_ref, high_ref):
    rows_dev = cond_ref.shape[0]
    source = row_source(halo, rows_dev, runs, (x_ref, cond_ref, top_ref, bottom_ref))
    deep = (rows_dev + 2 * halo) // ROW_SEGS
    half = ROW_SEGS * halo
    lane = lax.broadcasted_iota(jnp.int32, (runs + SUB, LANES), 1)
    for block in range(low_ref.shape[0]):
        low = jnp.zeros((runs + SUB, LANES), f32)
        high = jnp.zeros((runs + SUB, LANES), f32)
        for parity in range(2):
            if 2 * block + parity >= deep:
                break
            for seg in range(ROW_SEGS):
                value = source(seg * deep + 2 * block + parity, SUB)
                spot = parity * half + seg * halo
                here = (lane >= spot) & (lane < spot + halo)
                first = pltpu.roll(value, spot, 1) if spot else value
                shift = (spot + halo) % LANES
                last = pltpu.roll(value, shift, 1) if shift else value
                low = jnp.where(here, first, low)
                high = jnp.where(here, last, high)
        low_ref[block] = low
        high_ref[block] = high


LOSS_PIECES = 3
PIECES = 2


def pieces_of(x, count=PIECES):
    pieces = []
    for _ in range(count):
        pieces.append(x.astype(bf16))
        x = x - pieces[-1].astype(f32)
    return pieces


def tile_kernel(
    halo, steps, runs, x_ref, cond_ref, top_ref, bottom_ref, left_ref, right_ref, inverse_ref,
    counts_ref, main_ref, edge_ref, order_ref, decoder_hbm, out_ref, weights_hbm, u_ref, c_ref,
    rate_ref, body_ref, ends_ref, back_ref, decoder_ref, weights_ref, part_ref, sems,
):
    fetch = pltpu.make_async_copy(decoder_hbm, decoder_ref, sems.at[0])
    fetch.start()
    rows_dev, cols_dev = cond_ref.shape
    source = row_source(halo, rows_dev, runs, (x_ref, cond_ref, top_ref, bottom_ref))
    deep = (rows_dev + 2 * halo) // ROW_SEGS
    across = (cols_dev + 2 * halo) // COL_SEGS
    tall = runs + GROUP
    row_at, row_count = lax.axis_index("row"), lax.axis_size("row")
    col_at, col_count = lax.axis_index("col"), lax.axis_size("col")

    for b in range(deep):
        for seg in range(ROW_SEGS):
            for i, piece in enumerate(pieces_of(source(seg * deep + b, GROUP))):
                body_ref[i, b * tall : (b + 1) * tall, seg * cols_dev : (seg + 1) * cols_dev] = piece
        for side, ref in enumerate((left_ref, right_ref)):
            value = jnp.concatenate([ref[b // 2], ref[b // 2, runs:]], axis=0)
            for i, piece in enumerate(pieces_of(value)):
                first = b // 2 * tall
                ends_ref[i, b % 2, first : first + tall, side * LANES : (side + 1) * LANES] = piece

    lane = lax.broadcasted_iota(jnp.int32, (SUB, LANES), 1)
    chunk = 3 if across % 3 == 0 else 1
    for start in range(0, across, chunk):
        lanes = slice(start * LANES, (start + chunk) * LANES)
        total = None
        for i in range(PIECES):
            part = jnp.dot(body_ref[i], main_ref[:, lanes], preferred_element_type=f32)
            total = part if total is None else total + part
        extra = []
        for parity in range(2):
            more = None
            for i in range(PIECES):
                part = jnp.dot(
                    ends_ref[i, parity], edge_ref[parity, :, lanes], preferred_element_type=f32
                )
                more = part if more is None else more + part
            extra.append(more)
        for b in range(deep):
            first = b // 2 * tall
            value = total[b * tall : (b + 1) * tall] + extra[b % 2][first : first + tall]
            for inner in range(chunk):
                q = start + inner
                here = value[:, inner * LANES : (inner + 1) * LANES]
                u_ref[0, b, q] = here[:runs]
                c_ref[b + 1, q] = here[runs : runs + SUB]
    for b in range(deep):
        for q in range(across):
            row = lane // COL_SEGS * deep + b
            col = lane % COL_SEGS * across + q
            inside = (
                ((row >= halo) | (row_at > 0))
                & ((row < halo + rows_dev) | (row_at < row_count - 1))
                & ((col >= halo) | (col_at > 0))
                & ((col < halo + cols_dev) | (col_at < col_count - 1))
            )
            rate_ref[b, q] = jnp.where(inside, 0.5 * time_step, 0.0)
    for q in range(across):
        c_ref[0, q] = pltpu.roll(c_ref[deep, q], COL_SEGS, 1)
        c_ref[deep + 1, q] = pltpu.roll(c_ref[1, q], LANES - COL_SEGS, 1)

    size = part_ref.shape[1] // decoder_ref.shape[1]
    chunks = decoder_ref.shape[0] // size
    each = -(-chunks // (runs // SUB))
    fetch.wait()

    def group(index, _):
        where = pl.ds(pl.multiple_of(index * SUB, SUB), SUB)
        inverse = inverse_ref[where, :]
        counts = counts_ref[where, :]

        def step(number, old, new):
            active = jnp.where(number < counts, inverse, 0.0)

            def get(b, q):
                if b < 0:
                    u = pltpu.roll(u_ref[old, deep - 1, q, where, :], COL_SEGS, 1)
                elif b == deep:
                    u = pltpu.roll(u_ref[old, 0, q, where, :], LANES - COL_SEGS, 1)
                else:
                    u = u_ref[old, b, q, where, :]
                return u, kappa_of(u, c_ref[b + 1, q], inverse)

            last = [get(-1, q) for q in range(across)]
            here = [get(0, q) for q in range(across)]
            below = [(k0 + k1) * (u1 - u0) for (u0, k0), (u1, k1) in zip(last, here)]
            for b in range(deep):
                u = [pair[0] for pair in here]
                k = [pair[1] for pair in here]
                u.append(pltpu.roll(u[0], LANES - 1, 1))
                k.append(pltpu.roll(k[0], LANES - 1, 1))
                side = [(k[q] + k[q + 1]) * (u[q + 1] - u[q]) for q in range(across)]
                side.append(pltpu.roll(side[across - 1], 1, 1))
                then = [get(b + 1, q) for q in range(across)]
                above = [(k[q] + then[q][1]) * (then[q][0] - u[q]) for q in range(across)]
                for q in range(across):
                    flux = (above[q] - below[q]) + (side[q] - side[q - 1])
                    u_ref[new, b, q, where, :] = u[q] + (rate_ref[b, q] * active) * flux
                here, below = then, above

        done = 0
        for number in range(steps):
            step(number, number % 2, 1 - number % 2)
            while done < each * (number + 1) // steps:
                chunk = jnp.minimum(index * each + done, chunks - 1)
                reorder(chunk, size, decoder_ref, order_ref, weights_ref, part_ref)
                done += 1
        return 0

    lax.fori_loop(0, runs // SUB, group, 0)
    store = pltpu.make_async_copy(weights_ref, weights_hbm, sems.at[1])
    store.start()

    for b in range(deep):
        for q in range(across):
            for i, piece in enumerate(pieces_of(u_ref[steps % 2, b, q])):
                back_ref[i, b * runs : (b + 1) * runs, q * LANES : (q + 1) * LANES] = piece
    chunk = 2 if ROW_SEGS % 2 == 0 else 1
    for start in range(0, ROW_SEGS, chunk):
        places = slice(start * cols_dev, (start + chunk) * cols_dev)
        total = None
        for i in range(PIECES):
            part = lax.dot_general(
                back_ref[i], main_ref[places, :], (((1,), (1,)), ((), ())), preferred_element_type=f32
            )
            total = part if total is None else total + part
        for b in range(deep):
            for inner in range(chunk):
                row = (start + inner) * deep + b - halo
                if 0 <= row < rows_dev:
                    out_ref[pl.ds(row, runs, stride=rows_dev), :] = total[
                        b * runs : (b + 1) * runs, inner * cols_dev : (inner + 1) * cols_dev
                    ]
    store.wait()


def strip_kernel(halo, steps, runs, scale_of, *refs):
    count = lax.axis_size("col")
    blocks = refs[:count]
    order_ref, inverse_ref, counts_ref, hidden_ref, weights_hbm = refs[count : count + 5]
    out_ref, loss_ref, u_ref, c_ref, turned_ref, wide_ref = refs[count + 6 : count + 12]
    shot_ref, weights_ref, gram_ref, square_ref, sems = refs[count + 12 :]
    cols_dev = blocks[0].shape[2]
    wide = count * cols_dev
    parts = wide // LANES
    rows = u_ref.shape[0]
    band = rows - 2 * halo
    index = pl.program_id(0)
    col_at = lax.axis_index("col")
    row_at, row_count = lax.axis_index("row"), lax.axis_size("row")
    has_top = (row_at > 0) | (col_at > 0)
    has_bottom = (row_at < row_count - 1) | (col_at < count - 1)
    lane = lax.broadcasted_iota(jnp.int32, (GROUP, LANES), 1)
    first_lane, last_lane = lane == 0, lane == LANES - 1

    def ordered(get):
        whole = jnp.concatenate([get(block) for block in blocks], axis=1)
        return jnp.dot(whole, turned_ref[...], preferred_element_type=f32)

    groups = runs // GROUP
    each = -(-band // groups)
    cells = band * wide
    fetches = []
    for part in range(groups):
        lanes = slice(min(part * each * wide, cells), min((part + 1) * each * wide, cells))
        if lanes.start < lanes.stop:
            fetches.append(
                pltpu.make_async_copy(
                    weights_hbm.at[:, lanes], weights_ref.at[:, lanes], sems.at[part]
                )
            )

    @pl.when(index == 0)
    def _():
        for fetch in fetches:
            fetch.start()
        if weights_ref.shape[1] > cells:
            weights_ref[:, cells:] = jnp.zeros_like(weights_ref[:, cells:])
        gram_ref[...] = jnp.zeros_like(gram_ref)
        for back in range(count):
            at = lax.rem(col_at + count - back, count)
            turned_ref[back * cols_dev : (back + 1) * cols_dev, :] = order_ref[
                pl.ds(pl.multiple_of(at * cols_dev, cols_dev), cols_dev), :
            ]
        plane = ordered(lambda block: block[runs])
        for row in range(rows):
            c_ref[row] = jnp.broadcast_to(plane[row : row + 1], (SUB, wide))
        square_ref[...] = jnp.zeros_like(square_ref)

    for part, fetch in enumerate(fetches):
        pl.when(index == part)(fetch.wait)

    def split(x):
        return [x[..., part * LANES : (part + 1) * LANES] for part in range(parts)]

    where = pl.ds(pl.multiple_of(index * GROUP, GROUP), GROUP)
    fields = ordered(lambda block: block[where].reshape(GROUP * rows, cols_dev))
    for part, values in enumerate(split(fields)):
        wide_ref[part] = values
    for row in range(rows):
        for part in range(parts):
            lanes = pl.ds(part * LANES, LANES)
            u_ref[row, :, lanes] = wide_ref[part, pl.ds(row, GROUP, stride=rows), :]
    inverse = inverse_ref[where, :]
    counts = counts_ref[where, :]
    first_row = pl.multiple_of(index * GROUP * steps, GROUP)

    def get(row):
        u = split(u_ref[row])
        cond = split(jnp.concatenate([c_ref[row]] * (GROUP // SUB), axis=0))
        return u, [kappa_of(a, b, inverse) for a, b in zip(u, cond)]

    for number in range(steps):
        factor = jnp.where(number < counts, 0.5 * time_step * inverse, 0.0)
        top_scale = jnp.where(has_top, factor, 0.0)
        bottom_scale = jnp.where(has_bottom, factor, 0.0)

        def one(row, carry, scale, keep):
            u, k, below, square = carry
            then_u, then_k = get(row + 1)
            above = [(a + b) * (c - d) for a, b, c, d in zip(k, then_k, then_u, u)]
            u_more = u + [jnp.where(last_lane, 0.0, pltpu.roll(u[0], LANES - 1, 1))]
            k_more = k + [jnp.where(last_lane, 0.0, pltpu.roll(k[0], LANES - 1, 1))]
            side = [(k_more[p] + k_more[p + 1]) * (u_more[p + 1] - u_more[p]) for p in range(parts)]
            start = jnp.where(first_lane, k[0] * u[0], pltpu.roll(side[-1], 1, 1))
            side = [start] + side
            for p in range(parts):
                fresh = u[p] + scale * ((above[p] - below[p]) + (side[p + 1] - side[p]))
                u_ref[row, :, pl.ds(p * LANES, LANES)] = fresh
                if keep:
                    shot = fresh.astype(bf16)
                    lanes = pl.ds((row - halo) * wide + p * LANES, LANES)
                    shot_ref[pl.ds(first_row + number * GROUP, GROUP), lanes] = shot
                    again = shot.astype(f32)
                    square = square + again * again
            return then_u, then_k, above, square

        last_u, last_k = get(number)
        u, k = get(number + 1)
        below = [(a + b) * (c - d) for a, b, c, d in zip(k, last_k, u, last_u)]
        carry = (u, k, below, jnp.zeros((GROUP, LANES), f32))
        for row in range(number + 1, halo):
            carry = one(row, carry, top_scale, False)
        for row in range(halo, halo + band):
            carry = one(row, carry, factor, True)
        for row in range(halo + band, rows - 1 - number):
            carry = one(row, carry, bottom_scale, False)
        square_ref[...] += carry[3]
        for spare in range(each * number // steps, each * (number + 1) // steps):
            lanes = pl.ds(pl.multiple_of((index * each + spare) * wide, wide), wide)
            cell = weights_ref[:, lanes]
            gram_ref[...] += lax.dot_general(
                cell, cell, (((1,), (1,)), ((), ())), preferred_element_type=f32
            )

    @pl.when(index == pl.num_programs(0) - 1)
    def _():
        pushed = None
        for piece in pieces_of(gram_ref[...]):
            part = jnp.dot(hidden_ref[...], piece, preferred_element_type=f32)
            pushed = part if pushed is None else pushed + part
        drawn = product(shot_ref, weights_ref)
        out_ref[...] = ((pushed - drawn) * scale_of).astype(bf16)
        loss = jnp.sum(hidden_ref[...].astype(f32) * (pushed - 2.0 * drawn), axis=0, keepdims=True)
        loss_ref[...] = loss
        loss_ref[:, :LANES] += jnp.sum(square_ref[...], axis=0, keepdims=True)


def share_kernel(pieces_ref, loss_ref, out_ref):
    total = pieces_ref[0].astype(f32)
    for source in range(1, pieces_ref.shape[0]):
        total = total + pieces_ref[source].astype(f32)
    rows = [piece.astype(f32) for piece in pieces_of(loss_ref[...], LOSS_PIECES)]
    filler = jnp.zeros((out_ref.shape[1] - total.shape[0] - LOSS_PIECES, total.shape[1]), f32)
    message = jnp.concatenate([total] + rows + [filler], axis=0).astype(bf16)
    for target in range(out_ref.shape[0]):
        out_ref[target] = message


def finish_kernel(
    share, loss_scale, mine_ref, other_ref, act_ref, slope_ref, rows_ref, w_in_ref, bias_ref,
    w_out_ref, new_in_ref, new_bias_ref, new_out_ref, loss_ref, grad_ref, parts_ref,
):
    core = lax.axis_index("run")
    cells = mine_ref.shape[0]
    for at, ref in ((core, mine_ref), (1 - core, other_ref)):
        parts = jnp.zeros((1, ref.shape[2]), f32)
        rows = []
        for source in range(cells):
            value = ref[source].astype(f32)
            rows.append(value[:share])
            for piece in range(LOSS_PIECES):
                parts = parts + value[share + piece : share + piece + 1]
        size = cells * share
        grad_ref[pl.ds(pl.multiple_of(at * size, size), size), :] = jnp.concatenate(
            rows, axis=0
        ).astype(bf16)
        parts_ref[pl.ds(at, 1), :] = parts
    loss = jnp.sum(parts_ref[0:1] + parts_ref[1:2], axis=1, keepdims=True) * loss_scale
    loss_ref[...] = jnp.broadcast_to(loss, loss_ref.shape)
    grad = grad_ref[...]
    by_rows = (((0,), (0,)), ((), ()))
    grad_out = lax.dot_general(act_ref[...], grad, by_rows, preferred_element_type=f32)
    new_out_ref[...] = w_out_ref[...].astype(f32) - learn_rate * grad_out
    back = lax.dot_general(
        grad, w_out_ref[...], (((1,), (1,)), ((), ())), preferred_element_type=f32
    )
    grad_pre = back * slope_ref[...]
    new_bias_ref[...] = bias_ref[...] - learn_rate * jnp.sum(grad_pre, axis=0, keepdims=True)
    grad_in = lax.dot_general(
        rows_ref[...], grad_pre.astype(bf16), by_rows, preferred_element_type=f32
    )
    new_in_ref[...] = w_in_ref[...].astype(f32) - learn_rate * grad_in


def per_device(
    init_field, conduct, nonlin, counts, descriptors, time_code, w_in, bias_in, w_out, decoder
):
    runs, rows_dev, cols_dev = init_field.shape
    steps = time_code.shape[0]
    inputs, hidden_size = w_in.shape
    run_size = lax.axis_size("run")
    row_size = lax.axis_size("row")
    col_size = lax.axis_size("col")
    halo = steps
    band = rows_dev // col_size
    rows_strip = band + 2 * halo
    wide = cols_dev * col_size
    groups = runs // GROUP
    runs_total = runs * run_size
    rows_all = runs_total * steps
    scale_of = 1.0 / rows_all

    def vmem(mib):
        return pltpu.CompilerParams(vmem_limit_bytes=mib * 1024 * 1024)

    in_vmem = pl.BlockSpec(memory_space=pltpu.VMEM)
    anywhere = pl.BlockSpec(memory_space=pl.ANY)

    tile = jnp.concatenate([init_field, conduct[None]], axis=0)
    top, bottom = neighbours(tile[:, rows_dev - halo :], tile[:, :halo], "row")

    padded = jnp.concatenate([top, tile, bottom], axis=1).astype(bf16)
    col_at = lax.axis_index("col")

    def message(target):
        return lax.dynamic_slice_in_dim(padded, target * band, rows_strip, 1)

    messages = [message((col_at + hop) % col_size) for hop in range(col_size)]

    deep = (rows_dev + 2 * halo) // ROW_SEGS
    across = (cols_dev + 2 * halo) // COL_SEGS
    tall = runs + GROUP
    tile_args = (
        init_field.reshape(runs * rows_dev, cols_dev),
        conduct,
        top.reshape(-1, cols_dev),
        bottom.reshape(-1, cols_dev),
    )
    pack_shape = jax.ShapeDtypeStruct((-(-deep // 2), runs + SUB, LANES), f32)
    low, high = pl.pallas_call(
        functools.partial(pack_kernel, halo, runs),
        out_shape=(pack_shape, pack_shape),
        in_specs=[in_vmem] * 4,
        out_specs=(in_vmem, in_vmem),
        compiler_params=vmem(8),
        name="pack_columns",
    )(*tile_args)
    (low, high), messages = lax.optimization_barrier(((low, high), messages))
    left, right = neighbours(high, low, "col")
    blocks = messages[:1]
    for hop in range(1, col_size):
        pairs = [(i, (i + hop) % col_size) for i in range(col_size)]
        blocks.append(lax.ppermute(messages[hop], "col", pairs))

    inverse_wide = jnp.broadcast_to(1.0 / nonlin[:, None], (runs, LANES))
    counts_wide = jnp.broadcast_to(counts[:, None], (runs, LANES))
    order = apart(wide)
    field, weights = pl.pallas_call(
        functools.partial(tile_kernel, halo, steps, runs),
        out_shape=(
            jax.ShapeDtypeStruct((runs * rows_dev, cols_dev), f32),
            jax.ShapeDtypeStruct((hidden_size, band * wide), bf16),
        ),
        in_specs=[in_vmem] * 11 + [anywhere],
        out_specs=(in_vmem, anywhere),
        scratch_shapes=[
            pltpu.VMEM((2, deep, across, runs, LANES), f32),
            pltpu.VMEM((deep + 2, across, SUB, LANES), f32),
            pltpu.VMEM((deep, across, SUB, LANES), f32),
            pltpu.VMEM((PIECES, deep * tall, ROW_SEGS * cols_dev), bf16),
            pltpu.VMEM((PIECES, 2, -(-deep // 2) * tall, 2 * LANES), bf16),
            pltpu.VMEM((PIECES, deep * runs, across * LANES), bf16),
            pltpu.VMEM(decoder.shape, bf16),
            pltpu.VMEM((hidden_size, band * wide), bf16),
            pltpu.VMEM((wide // LANES, 32 * band, LANES), f32),
            pltpu.SemaphoreType.DMA((2,)),
        ],
        compiler_params=vmem(48),
        cost_estimate=pl.CostEstimate(flops=10**11, bytes_accessed=10**7, transcendentals=0),
        name="tile_solver",
    )(*tile_args, left, right, inverse_wide, counts_wide, *tile_order(halo, cols_dev), order, decoder)
    final_field = field.reshape(init_field.shape)

    desc = descriptors.astype(f32).reshape(run_size * groups, 1, GROUP, -1)
    codes = time_code.astype(f32)[None, :, None, :]
    rows_in = (desc + codes).astype(bf16).reshape(rows_all, -1)
    pre = jnp.dot(rows_in, w_in, preferred_element_type=f32) + bias_in
    act, pull = jax.vjp(jax.nn.gelu, pre)
    slope = pull(jnp.ones_like(pre))[0]
    act = act.astype(bf16)
    hidden = jnp.dot(act, w_out, preferred_element_type=f32).astype(bf16)
    hidden, slope = lax.optimization_barrier((hidden, slope))
    mine = lax.dynamic_slice_in_dim(hidden, lax.axis_index("run") * runs * steps, runs * steps, 0)

    partial, loss = pl.pallas_call(
        functools.partial(strip_kernel, halo, steps, runs, scale_of),
        grid=(groups,),
        out_shape=(
            jax.ShapeDtypeStruct((runs * steps, hidden_size), bf16),
            jax.ShapeDtypeStruct((1, hidden_size), f32),
        ),
        in_specs=[in_vmem] * (col_size + 4) + [anywhere] * 2,
        out_specs=(in_vmem, in_vmem),
        scratch_shapes=[
            pltpu.VMEM((rows_strip, GROUP, wide), f32),
            pltpu.VMEM((rows_strip, SUB, wide), f32),
            pltpu.VMEM((wide, wide), bf16),
            pltpu.VMEM((wide // LANES, GROUP * rows_strip, LANES), f32),
            pltpu.VMEM((runs * steps, band * wide), bf16),
            pltpu.VMEM((hidden_size, -(-band // groups) * groups * wide), bf16),
            pltpu.VMEM((hidden_size, hidden_size), f32),
            pltpu.VMEM((GROUP, LANES), f32),
            pltpu.SemaphoreType.DMA((groups,)),
        ],
        compiler_params=vmem(40),
        name="strip_solver",
    )(*blocks, order, inverse_wide, counts_wide, mine, weights, field)

    cells = row_size * col_size
    share = runs * steps // cells
    pieces = lax.all_to_all(
        partial.reshape(cells, share, hidden_size), ("row", "col"), 0, 0, tiled=True
    )
    taller = -(-(share + LOSS_PIECES) // 16) * 16
    message_out = pl.pallas_call(
        share_kernel,
        out_shape=jax.ShapeDtypeStruct((cells, taller, hidden_size), bf16),
        in_specs=[in_vmem] * 2,
        out_specs=in_vmem,
        compiler_params=vmem(8),
        name="share_sum",
    )(pieces, loss)
    gathered = lax.all_to_all(message_out, ("row", "col"), 0, 0, tiled=True)
    swap = [(i, (i + 1) % run_size) for i in range(run_size)]
    other = lax.ppermute(gathered, "run", swap)
    cells_total = rows_dev * row_size * wide
    new_w_in, new_bias, new_w_out, mean_loss = pl.pallas_call(
        functools.partial(finish_kernel, share, 1.0 / (rows_all * cells_total)),
        out_shape=(
            jax.ShapeDtypeStruct((inputs, hidden_size), f32),
            jax.ShapeDtypeStruct((1, hidden_size), f32),
            jax.ShapeDtypeStruct((hidden_size, hidden_size), f32),
            jax.ShapeDtypeStruct((1, LANES), f32),
        ),
        in_specs=[in_vmem] * 8,
        out_specs=(in_vmem,) * 4,
        scratch_shapes=[
            pltpu.VMEM((rows_all, hidden_size), bf16),
            pltpu.VMEM((run_size, hidden_size), f32),
        ],
        compiler_params=vmem(16),
        name="trunk_update",
    )(gathered, other, act, slope, rows_in, w_in, bias_in[None], w_out)
    return (final_field, new_w_in, new_bias[0], new_w_out, mean_loss[0, 0])


def solution(mesh):
    in_specs = (
        P("run", "row", "col"),
        P("row", "col"),
        P("run"),
        P("run"),
        P(),
        P(),
        P(),
        P(),
        P(),
        P(None, ("row", "col"), None),
    )
    out_specs = (P("run", "row", "col"), P(), P(), P(), P())
    return jax.shard_map(
        per_device, mesh=mesh, in_specs=in_specs, out_specs=out_specs, check_vma=False
    )
```

```python
import functools

import jax
import jax.numpy as jnp
import numpy as np
from jax import lax
from jax.experimental import pallas as pl
from jax.experimental.pallas import tpu as pltpu
from jax.sharding import PartitionSpec as P

time_step = 0.12
learn_rate = 0.5
LANES = 128
FRONT_PARTS = 2
SUB = 8
GROUP = 16
f32 = jnp.float32
bf16 = jnp.bfloat16


def neighbours(up, down, axis):
    count = lax.axis_size(axis)
    forward = [(i, i + 1) for i in range(count - 1)]
    backward = [(target, source) for source, target in forward]
    return lax.ppermute(up, axis, forward), lax.ppermute(down, axis, backward)


def kappa_of(u, cond, inverse):
    return cond * pltpu.reciprocal(inverse + u * u, approx=True)


def spread(ref, first, count):
    at = lax.broadcasted_iota(jnp.int32, (count, LANES), 0)
    value = jnp.full((count, LANES), ref[first])
    for i in range(1, count):
        value = jnp.where(at == i, ref[first + i], value)
    return value


def apart(wide):
    parts = wide // LANES
    source = np.arange(wide)[:, None]
    place = np.arange(wide)[None, :]
    return jnp.asarray(source == parts * (place % LANES) + place // LANES, bf16)


def reorder(source, target, size, d_ref, order_ref, out_ref, wide_ref):
    _, band, wide = d_ref.shape
    here = pl.ds(pl.multiple_of(target * size, size), size)
    x = d_ref[pl.ds(pl.multiple_of(source * size, size), size)]
    if band % 16:
        x = x.astype(f32).reshape(size * band, wide).astype(bf16)
    else:
        x = x.reshape(size * band, wide)
    y = jnp.dot(x, order_ref[...], preferred_element_type=f32)
    for part in range(wide // LANES):
        wide_ref[part] = y[:, part * LANES : (part + 1) * LANES]
    for row in range(band):
        for part in range(wide // LANES):
            lanes = pl.ds(row * wide + part * LANES, LANES)
            out_ref[here, lanes] = wide_ref[part, pl.ds(row, size, stride=band), :].astype(bf16)


def product(left_ref, right_ref):
    cells = left_ref.shape[1]
    size = min(cells, 2048)
    total = None
    for start in range(0, cells, size):
        part = lax.dot_general(
            left_ref[:, start : start + size],
            right_ref[:, start : start + size],
            (((1,), (1,)), ((), ())),
            preferred_element_type=f32,
        )
        total = part if total is None else total + part
    return total


ROW_SEGS = 8
COND_ROWS = 16
COL_SEGS = 16


def tile_order(halo, cols_dev):
    across = (cols_dev + 2 * halo) // COL_SEGS
    lanes = ROW_SEGS * COL_SEGS
    place = np.arange(across * lanes)
    column = (place % COL_SEGS) * across + place // lanes
    seg_row = (place % lanes) // COL_SEGS
    source = np.arange(ROW_SEGS * cols_dev)[:, None]
    main = (source // cols_dev == seg_row) & (source % cols_dev + halo == column)
    half = ROW_SEGS * halo
    parity = np.arange(2)[:, None, None, None]
    high = np.arange(2)[:, None, None]
    source = np.arange(LANES)[:, None]
    edge = (
        (source // half == parity)
        & (source % half // halo == seg_row)
        & (source % halo + high * (cols_dev + halo) == column)
    )
    return jnp.asarray(main, bf16), jnp.asarray(edge.reshape(2, 2 * LANES, -1), bf16)


def row_source(halo, rows_dev, runs, refs):
    x_ref, cond_ref, top_ref, bottom_ref = refs

    def source(row):
        if row < halo:
            return top_ref[pl.ds(row, runs, stride=halo), :], top_ref[pl.ds(runs * halo + row, 1), :]
        row -= halo
        if row < rows_dev:
            return x_ref[pl.ds(row, runs, stride=rows_dev), :], cond_ref[pl.ds(row, 1), :]
        row -= rows_dev
        return (
            bottom_ref[pl.ds(row, runs, stride=halo), :],
            bottom_ref[pl.ds(runs * halo + row, 1), :],
        )

    def both(row, copies):
        runs_of, cond = source(row)
        return jnp.concatenate([runs_of, jnp.broadcast_to(cond, (copies, LANES))], axis=0)

    return both


def pack_kernel(halo, runs, x_ref, cond_ref, top_ref, bottom_ref, low_ref, high_ref):
    rows_dev = cond_ref.shape[0]
    source = row_source(halo, rows_dev, runs, (x_ref, cond_ref, top_ref, bottom_ref))
    deep = (rows_dev + 2 * halo) // ROW_SEGS
    half = ROW_SEGS * halo
    lane = lax.broadcasted_iota(jnp.int32, (runs + SUB, LANES), 1)
    for block in range(low_ref.shape[0]):
        low = jnp.zeros((runs + SUB, LANES), f32)
        high = jnp.zeros((runs + SUB, LANES), f32)
        for parity in range(2):
            if 2 * block + parity >= deep:
                break
            for seg in range(ROW_SEGS):
                value = source(seg * deep + 2 * block + parity, SUB)
                spot = parity * half + seg * halo
                here = (lane >= spot) & (lane < spot + halo)
                first = pltpu.roll(value, spot, 1) if spot else value
                shift = (spot + halo) % LANES
                last = pltpu.roll(value, shift, 1) if shift else value
                low = jnp.where(here, first, low)
                high = jnp.where(here, last, high)
        low_ref[block] = low
        high_ref[block] = high


LOSS_PIECES = 3
PIECES = 2


def pieces_of(x, count=PIECES):
    pieces = []
    for _ in range(count):
        pieces.append(x.astype(bf16))
        x = x - pieces[-1].astype(f32)
    return pieces


def tile_kernel(part, halo, steps, runs, *refs):
    x_ref, cond_ref, top_ref, bottom_ref, left_ref, right_ref, nonlin_ref, counts_ref = refs[:8]
    main_ref, edge_ref = refs[8:10]
    out_ref, u_ref, c_ref, rate_ref, body_ref, ends_ref, back_ref, pad_ref = refs[-8:]
    rows_dev, cols_dev = cond_ref.shape
    deep = (rows_dev + 2 * halo) // ROW_SEGS
    across = (cols_dev + 2 * halo) // COL_SEGS
    packs = left_ref.shape[0]
    first_run = part * GROUP
    row_at, row_count = lax.axis_index("row"), lax.axis_size("row")
    col_at, col_count = lax.axis_index("col"), lax.axis_size("col")

    def source(row):
        if row < halo:
            return top_ref[pl.ds(first_run * halo + row, GROUP, stride=halo), :]
        row -= halo
        if row < rows_dev:
            return x_ref[pl.ds(row, GROUP, stride=rows_dev), :]
        return bottom_ref[pl.ds(first_run * halo + row - rows_dev, GROUP, stride=halo), :]

    pad_ref[...] = jnp.zeros_like(pad_ref)
    pad_ref[:halo] = top_ref[runs * halo : (runs + 1) * halo]
    pad_ref[halo : halo + rows_dev] = cond_ref[...]
    pad_ref[halo + rows_dev : 2 * halo + rows_dev] = bottom_ref[runs * halo : (runs + 1) * halo]
    for seg in range(ROW_SEGS):
        lanes = slice(seg * cols_dev, (seg + 1) * cols_dev)
        for b in range(deep):
            for i, piece in enumerate(pieces_of(source(seg * deep + b))):
                body_ref[i, b * GROUP : (b + 1) * GROUP, lanes] = piece
        for i, piece in enumerate(pieces_of(pad_ref[seg * deep : seg * deep + COND_ROWS])):
            body_ref[i, deep * GROUP : deep * GROUP + COND_ROWS, lanes] = piece
    for side, ref in enumerate((left_ref, right_ref)):
        lanes = slice(side * LANES, (side + 1) * LANES)
        for block in range(packs):
            for i, piece in enumerate(pieces_of(ref[block, first_run : first_run + GROUP])):
                ends_ref[i, block * GROUP : (block + 1) * GROUP, lanes] = piece
        conds = [ref[block, runs : runs + 1] for block in range(packs)]
        conds.append(jnp.zeros((COND_ROWS - packs, LANES), f32))
        for i, piece in enumerate(pieces_of(jnp.concatenate(conds, axis=0))):
            ends_ref[i, packs * GROUP : packs * GROUP + COND_ROWS, lanes] = piece

    lane = lax.broadcasted_iota(jnp.int32, (SUB, LANES), 1)
    chunk = 3 if across % 3 == 0 else 1
    for start in range(0, across, chunk):
        lanes = slice(start * LANES, (start + chunk) * LANES)
        total = None
        extra = [None, None]
        for i in range(PIECES):
            more = jnp.dot(body_ref[i], main_ref[:, lanes], preferred_element_type=f32)
            total = more if total is None else total + more
            for parity in range(2):
                more = jnp.dot(ends_ref[i], edge_ref[parity, :, lanes], preferred_element_type=f32)
                extra[parity] = more if extra[parity] is None else extra[parity] + more
        for b in range(deep):
            first = b // 2 * GROUP
            value = total[b * GROUP : (b + 1) * GROUP] + extra[b % 2][first : first + GROUP]
            at = packs * GROUP + b // 2
            cond = total[deep * GROUP + b : deep * GROUP + b + 1] + extra[b % 2][at : at + 1]
            for inner in range(chunk):
                q = start + inner
                here = slice(inner * LANES, (inner + 1) * LANES)
                u_ref[0, b, q] = value[:, here]
                c_ref[b + 1, q] = jnp.broadcast_to(cond[:, here], (SUB, LANES))
    for b in range(deep):
        for q in range(across):
            row = lane // COL_SEGS * deep + b
            col = lane % COL_SEGS * across + q
            inside = (
                ((row >= halo) | (row_at > 0))
                & ((row < halo + rows_dev) | (row_at < row_count - 1))
                & ((col >= halo) | (col_at > 0))
                & ((col < halo + cols_dev) | (col_at < col_count - 1))
            )
            rate_ref[b, q] = jnp.where(inside, 0.5 * time_step, 0.0)
    for q in range(across):
        c_ref[0, q] = pltpu.roll(c_ref[deep, q], COL_SEGS, 1)
        c_ref[deep + 1, q] = pltpu.roll(c_ref[1, q], LANES - COL_SEGS, 1)

    def group(index, _):
        where = pl.ds(pl.multiple_of(index * SUB, SUB), SUB)
        inverse = 1.0 / spread(nonlin_ref, first_run + index * SUB, SUB)
        counts = spread(counts_ref, first_run + index * SUB, SUB)

        def step(number, old, new):
            active = jnp.where(number < counts, inverse, 0.0)

            def get(b, q):
                if b < 0:
                    u = pltpu.roll(u_ref[old, deep - 1, q, where, :], COL_SEGS, 1)
                elif b == deep:
                    u = pltpu.roll(u_ref[old, 0, q, where, :], LANES - COL_SEGS, 1)
                else:
                    u = u_ref[old, b, q, where, :]
                return u, kappa_of(u, c_ref[b + 1, q], inverse)

            last = [get(-1, q) for q in range(across)]
            here = [get(0, q) for q in range(across)]
            below = [(k0 + k1) * (u1 - u0) for (u0, k0), (u1, k1) in zip(last, here)]
            for b in range(deep):
                u = [pair[0] for pair in here]
                k = [pair[1] for pair in here]
                u.append(pltpu.roll(u[0], LANES - 1, 1))
                k.append(pltpu.roll(k[0], LANES - 1, 1))
                side = [(k[q] + k[q + 1]) * (u[q + 1] - u[q]) for q in range(across)]
                side.append(pltpu.roll(side[across - 1], 1, 1))
                then = [get(b + 1, q) for q in range(across)]
                above = [(k[q] + then[q][1]) * (then[q][0] - u[q]) for q in range(across)]
                for q in range(across):
                    flux = (above[q] - below[q]) + (side[q] - side[q - 1])
                    u_ref[new, b, q, where, :] = u[q] + (rate_ref[b, q] * active) * flux
                here, below = then, above

        def two(i, _):
            step(2 * i, 0, 1)
            step(2 * i + 1, 1, 0)
            return 0

        lax.fori_loop(0, steps // 2, two, 0)
        return 0

    lax.fori_loop(0, GROUP // SUB, group, 0)

    for b in range(deep):
        for q in range(across):
            for i, piece in enumerate(pieces_of(u_ref[0, b, q])):
                back_ref[i, b * GROUP : (b + 1) * GROUP, q * LANES : (q + 1) * LANES] = piece
    chunk = 2 if ROW_SEGS % 2 == 0 else 1
    for start in range(0, ROW_SEGS, chunk):
        places = slice(start * cols_dev, (start + chunk) * cols_dev)
        total = None
        for i in range(PIECES):
            more = lax.dot_general(
                back_ref[i], main_ref[places, :], (((1,), (1,)), ((), ())), preferred_element_type=f32
            )
            total = more if total is None else total + more
        for b in range(deep):
            for inner in range(chunk):
                row = (start + inner) * deep + b - halo
                if 0 <= row < rows_dev:
                    out_ref[pl.ds(row, GROUP, stride=rows_dev), :] = total[
                        b * GROUP : (b + 1) * GROUP, inner * cols_dev : (inner + 1) * cols_dev
                    ]


def decoder_kernel(d_ref, order_ref, out_ref, wide_ref):
    reorder(0, 0, d_ref.shape[0], d_ref, order_ref, out_ref, wide_ref)


def strip_kernel(halo, steps, runs, scale_of, *refs):
    count = lax.axis_size("col")
    blocks = refs[:count]
    order_ref, nonlin_ref, counts_ref, hidden_ref, weights_hbm = refs[count : count + 5]
    out_ref, loss_ref, u_ref, c_ref, turned_ref, wide_ref = refs[count + 5 : count + 11]
    shot_ref, weights_ref, gram_ref, square_ref, sems = refs[count + 11 :]
    cols_dev = blocks[0].shape[2]
    wide = count * cols_dev
    parts = wide // LANES
    rows = u_ref.shape[0]
    band = rows - 2 * halo
    index = pl.program_id(0)
    col_at = lax.axis_index("col")
    row_at, row_count = lax.axis_index("row"), lax.axis_size("row")
    has_top = (row_at > 0) | (col_at > 0)
    has_bottom = (row_at < row_count - 1) | (col_at < count - 1)
    lane = lax.broadcasted_iota(jnp.int32, (GROUP, LANES), 1)
    first_lane, last_lane = lane == 0, lane == LANES - 1

    def ordered(get):
        whole = jnp.concatenate([get(block) for block in blocks], axis=1)
        return jnp.dot(whole, turned_ref[...], preferred_element_type=f32)

    groups = runs // GROUP
    each = -(-band // groups)
    cells = band * wide
    fetches = []
    for part in range(groups):
        lanes = slice(min(part * each * wide, cells), min((part + 1) * each * wide, cells))
        if lanes.start < lanes.stop:
            fetches.append(
                pltpu.make_async_copy(
                    weights_hbm.at[:, lanes], weights_ref.at[:, lanes], sems.at[part]
                )
            )

    @pl.when(index == 0)
    def _():
        for fetch in fetches:
            fetch.start()
        if weights_ref.shape[1] > cells:
            weights_ref[:, cells:] = jnp.zeros_like(weights_ref[:, cells:])
        gram_ref[...] = jnp.zeros_like(gram_ref)
        for back in range(count):
            at = lax.rem(col_at + count - back, count)
            turned_ref[back * cols_dev : (back + 1) * cols_dev, :] = order_ref[
                pl.ds(pl.multiple_of(at * cols_dev, cols_dev), cols_dev), :
            ]
        plane = ordered(lambda block: block[runs])
        for row in range(rows):
            c_ref[row] = jnp.broadcast_to(plane[row : row + 1], (SUB, wide))
        square_ref[...] = jnp.zeros_like(square_ref)

    for part, fetch in enumerate(fetches):
        pl.when(index == part)(fetch.wait)

    def split(x):
        return [x[..., part * LANES : (part + 1) * LANES] for part in range(parts)]

    where = pl.ds(pl.multiple_of(index * GROUP, GROUP), GROUP)
    fields = ordered(lambda block: block[where].reshape(GROUP * rows, cols_dev))
    for part, values in enumerate(split(fields)):
        wide_ref[part] = values
    for row in range(rows):
        for part in range(parts):
            lanes = pl.ds(part * LANES, LANES)
            u_ref[row, :, lanes] = wide_ref[part, pl.ds(row, GROUP, stride=rows), :]
    inverse = 1.0 / spread(nonlin_ref, index * GROUP, GROUP)
    counts = spread(counts_ref, index * GROUP, GROUP)
    first_row = pl.multiple_of(index * GROUP * steps, GROUP)

    def get(row):
        u = split(u_ref[row])
        cond = split(jnp.concatenate([c_ref[row]] * (GROUP // SUB), axis=0))
        return u, [kappa_of(a, b, inverse) for a, b in zip(u, cond)]

    for number in range(steps):
        factor = jnp.where(number < counts, 0.5 * time_step * inverse, 0.0)
        top_scale = jnp.where(has_top, factor, 0.0)
        bottom_scale = jnp.where(has_bottom, factor, 0.0)

        def one(row, carry, scale, keep):
            u, k, below, square = carry
            then_u, then_k = get(row + 1)
            above = [(a + b) * (c - d) for a, b, c, d in zip(k, then_k, then_u, u)]
            u_more = u + [jnp.where(last_lane, 0.0, pltpu.roll(u[0], LANES - 1, 1))]
            k_more = k + [jnp.where(last_lane, 0.0, pltpu.roll(k[0], LANES - 1, 1))]
            side = [(k_more[p] + k_more[p + 1]) * (u_more[p + 1] - u_more[p]) for p in range(parts)]
            start = jnp.where(first_lane, k[0] * u[0], pltpu.roll(side[-1], 1, 1))
            side = [start] + side
            for p in range(parts):
                fresh = u[p] + scale * ((above[p] - below[p]) + (side[p + 1] - side[p]))
                u_ref[row, :, pl.ds(p * LANES, LANES)] = fresh
                if keep:
                    shot = fresh.astype(bf16)
                    lanes = pl.ds((row - halo) * wide + p * LANES, LANES)
                    shot_ref[pl.ds(first_row + number * GROUP, GROUP), lanes] = shot
                    again = shot.astype(f32)
                    square = square + again * again
            return then_u, then_k, above, square

        last_u, last_k = get(number)
        u, k = get(number + 1)
        below = [(a + b) * (c - d) for a, b, c, d in zip(k, last_k, u, last_u)]
        carry = (u, k, below, jnp.zeros((GROUP, LANES), f32))
        for row in range(number + 1, halo):
            carry = one(row, carry, top_scale, False)
        for row in range(halo, halo + band):
            carry = one(row, carry, factor, True)
        for row in range(halo + band, rows - 1 - number):
            carry = one(row, carry, bottom_scale, False)
        square_ref[...] += carry[3]
        for spare in range(each * number // steps, each * (number + 1) // steps):
            lanes = pl.ds(pl.multiple_of((index * each + spare) * wide, wide), wide)
            cell = weights_ref[:, lanes]
            gram_ref[...] += lax.dot_general(
                cell, cell, (((1,), (1,)), ((), ())), preferred_element_type=f32
            )

    @pl.when(index == pl.num_programs(0) - 1)
    def _():
        size = runs * steps
        hidden = hidden_ref[pl.ds(pl.multiple_of(lax.axis_index("run") * size, size), size), :]
        pushed = None
        for piece in pieces_of(gram_ref[...]):
            part = jnp.dot(hidden, piece, preferred_element_type=f32)
            pushed = part if pushed is None else pushed + part
        drawn = product(shot_ref, weights_ref)
        out_ref[...] = ((pushed - drawn) * scale_of).astype(bf16)
        loss = jnp.sum(hidden.astype(f32) * (pushed - 2.0 * drawn), axis=0, keepdims=True)
        loss_ref[...] = loss
        loss_ref[:, :LANES] += jnp.sum(square_ref[...], axis=0, keepdims=True)


def share_kernel(pieces_ref, loss_ref, out_ref):
    total = pieces_ref[0].astype(f32)
    for source in range(1, pieces_ref.shape[0]):
        total = total + pieces_ref[source].astype(f32)
    rows = [piece.astype(f32) for piece in pieces_of(loss_ref[...], LOSS_PIECES)]
    filler = jnp.zeros((out_ref.shape[1] - total.shape[0] - LOSS_PIECES, total.shape[1]), f32)
    message = jnp.concatenate([total] + rows + [filler], axis=0).astype(bf16)
    for target in range(out_ref.shape[0]):
        out_ref[target] = message


def finish_kernel(
    share, loss_scale, mine_ref, other_ref, act_ref, slope_ref, rows_ref, w_in_ref, bias_ref,
    w_out_ref, new_in_ref, new_bias_ref, new_out_ref, loss_ref, grad_ref, parts_ref,
):
    core = lax.axis_index("run")
    cells = mine_ref.shape[0]
    for at, ref in ((core, mine_ref), (1 - core, other_ref)):
        parts = jnp.zeros((1, ref.shape[2]), f32)
        rows = []
        for source in range(cells):
            value = ref[source].astype(f32)
            rows.append(value[:share])
            for piece in range(LOSS_PIECES):
                parts = parts + value[share + piece : share + piece + 1]
        size = cells * share
        grad_ref[pl.ds(pl.multiple_of(at * size, size), size), :] = jnp.concatenate(
            rows, axis=0
        ).astype(bf16)
        parts_ref[pl.ds(at, 1), :] = parts
    loss = jnp.sum(parts_ref[0:1] + parts_ref[1:2], axis=1, keepdims=True) * loss_scale
    loss_ref[...] = jnp.broadcast_to(loss, loss_ref.shape)
    grad = grad_ref[...]
    by_rows = (((0,), (0,)), ((), ()))
    grad_out = lax.dot_general(act_ref[...], grad, by_rows, preferred_element_type=f32)
    new_out_ref[...] = w_out_ref[...].astype(f32) - learn_rate * grad_out
    back = lax.dot_general(
        grad, w_out_ref[...], (((1,), (1,)), ((), ())), preferred_element_type=f32
    )
    grad_pre = back * slope_ref[...]
    new_bias_ref[...] = bias_ref[...] - learn_rate * jnp.sum(grad_pre, axis=0, keepdims=True)
    grad_in = lax.dot_general(
        rows_ref[...], grad_pre.astype(bf16), by_rows, preferred_element_type=f32
    )
    new_in_ref[...] = w_in_ref[...].astype(f32) - learn_rate * grad_in


def per_device(
    init_field, conduct, nonlin, counts, descriptors, time_code, w_in, bias_in, w_out, decoder
):
    runs, rows_dev, cols_dev = init_field.shape
    steps = time_code.shape[0]
    inputs, hidden_size = w_in.shape
    run_size = lax.axis_size("run")
    row_size = lax.axis_size("row")
    col_size = lax.axis_size("col")
    halo = steps
    band = rows_dev // col_size
    rows_strip = band + 2 * halo
    wide = cols_dev * col_size
    groups = runs // GROUP
    runs_total = runs * run_size
    rows_all = runs_total * steps
    scale_of = 1.0 / rows_all

    def vmem(mib):
        return pltpu.CompilerParams(vmem_limit_bytes=mib * 1024 * 1024)

    in_vmem = pl.BlockSpec(memory_space=pltpu.VMEM)
    in_hbm = pl.BlockSpec(memory_space=pltpu.HBM)
    in_smem = pl.BlockSpec(memory_space=pltpu.SMEM)

    tile = jnp.concatenate([init_field, conduct[None]], axis=0)
    top, bottom = neighbours(tile[:, rows_dev - halo :], tile[:, :halo], "row")

    padded = jnp.concatenate([top, tile, bottom], axis=1).astype(bf16)
    col_at = lax.axis_index("col")

    def message(target):
        return lax.dynamic_slice_in_dim(padded, target * band, rows_strip, 1)

    messages = [message((col_at + hop) % col_size) for hop in range(col_size)]

    deep = (rows_dev + 2 * halo) // ROW_SEGS
    across = (cols_dev + 2 * halo) // COL_SEGS
    tile_args = (
        init_field.reshape(runs * rows_dev, cols_dev),
        conduct,
        top.reshape(-1, cols_dev),
        bottom.reshape(-1, cols_dev),
    )
    pack_shape = jax.ShapeDtypeStruct((-(-deep // 2), runs + SUB, LANES), f32)
    low, high = pl.pallas_call(
        functools.partial(pack_kernel, halo, runs),
        out_shape=(pack_shape, pack_shape),
        in_specs=[in_vmem] * 4,
        out_specs=(in_vmem, in_vmem),
        compiler_params=vmem(6),
        name="pack_columns",
    )(*tile_args)
    order = apart(wide)
    (low, high, order), messages = lax.optimization_barrier(((low, high, order), messages))
    left, right = neighbours(high, low, "col")
    blocks = messages[:1]
    for hop in range(1, col_size):
        pairs = [(i, (i + hop) % col_size) for i in range(col_size)]
        blocks.append(lax.ppermute(messages[hop], "col", pairs))

    size = 64
    weights = pl.pallas_call(
        decoder_kernel,
        grid=(hidden_size // size,),
        out_shape=jax.ShapeDtypeStruct((hidden_size, band * wide), bf16),
        in_specs=[pl.BlockSpec((size, band, wide), lambda i: (i, 0, 0)), in_vmem],
        out_specs=pl.BlockSpec((size, band * wide), lambda i: (i, 0)),
        scratch_shapes=[pltpu.VMEM((wide // LANES, size * band, LANES), f32)],
        compiler_params=vmem(12),
        cost_estimate=pl.CostEstimate(flops=10**10, bytes_accessed=10**7, transcendentals=0),
        name="decoder_order",
    )(decoder, order)

    main, edge = tile_order(halo, cols_dev)

    def solve(part, left, right, done):
        block = pl.BlockSpec((GROUP * rows_dev, cols_dev), lambda i: (part, 0))
        packs = left.shape[0]
        return pl.pallas_call(
            functools.partial(tile_kernel, part, halo, steps, runs),
            grid=(1,),
            out_shape=jax.ShapeDtypeStruct((runs * rows_dev, cols_dev), f32),
            in_specs=[block] + [in_vmem] * 5 + [in_smem] * 2 + [in_vmem] * 2 + [in_hbm] * len(done),
            out_specs=block,
            scratch_shapes=[
                pltpu.VMEM((2, deep, across, GROUP, LANES), f32),
                pltpu.VMEM((deep + 2, across, SUB, LANES), f32),
                pltpu.VMEM((deep, across, SUB, LANES), f32),
                pltpu.VMEM((PIECES, deep * GROUP + COND_ROWS, ROW_SEGS * cols_dev), bf16),
                pltpu.VMEM((PIECES, packs * GROUP + COND_ROWS, 2 * LANES), bf16),
                pltpu.VMEM((PIECES, deep * GROUP, across * LANES), bf16),
                pltpu.VMEM((rows_dev + 2 * halo + COND_ROWS, cols_dev), f32),
            ],
            input_output_aliases={10: 0} if done else {},
            compiler_params=vmem(14),
            cost_estimate=pl.CostEstimate(
                flops=10**10 if done else 10**11, bytes_accessed=10**7, transcendentals=0
            ),
            name="tile_solver",
        )(*tile_args, left, right, nonlin, counts, main, edge, *done)

    early = FRONT_PARTS
    field = ()
    for part in range(early):
        field = (solve(part, left, right, field),)

    desc = descriptors.astype(f32).reshape(run_size * groups, 1, GROUP, -1)
    codes = time_code.astype(f32)[None, :, None, :]
    rows_in = (desc + codes).astype(bf16).reshape(rows_all, -1)
    pre = jnp.dot(rows_in, w_in, preferred_element_type=f32) + bias_in
    act, pull = jax.vjp(jax.nn.gelu, pre)
    slope = pull(jnp.ones_like(pre))[0]
    act = act.astype(bf16)
    hidden = jnp.dot(act, w_out, preferred_element_type=f32).astype(bf16)
    hidden, slope = lax.optimization_barrier((hidden, slope))
    hidden, *field = lax.optimization_barrier((hidden, *field))
    partial, loss = pl.pallas_call(
        functools.partial(strip_kernel, halo, steps, runs, scale_of),
        grid=(groups,),
        out_shape=(
            jax.ShapeDtypeStruct((runs * steps, hidden_size), bf16),
            jax.ShapeDtypeStruct((1, hidden_size), f32),
        ),
        in_specs=[in_vmem] * (col_size + 1) + [in_smem] * 2 + [in_vmem, in_hbm],
        out_specs=(in_vmem, in_vmem),
        scratch_shapes=[
            pltpu.VMEM((rows_strip, GROUP, wide), f32),
            pltpu.VMEM((rows_strip, SUB, wide), f32),
            pltpu.VMEM((wide, wide), bf16),
            pltpu.VMEM((wide // LANES, GROUP * rows_strip, LANES), f32),
            pltpu.VMEM((runs * steps, band * wide), bf16),
            pltpu.VMEM((hidden_size, -(-band // groups) * groups * wide), bf16),
            pltpu.VMEM((hidden_size, hidden_size), f32),
            pltpu.VMEM((GROUP, LANES), f32),
            pltpu.SemaphoreType.DMA((groups,)),
        ],
        compiler_params=vmem(30),
        name="strip_solver",
    )(*blocks, order, nonlin, counts, hidden, weights)

    cells = row_size * col_size
    share = runs * steps // cells
    partial, left, right = lax.optimization_barrier((partial, left, right))
    for part in range(early, groups - 1):
        field = (solve(part, left, right, field),)
    pieces = lax.all_to_all(
        partial.reshape(cells, share, hidden_size), ("row", "col"), 0, 0, tiled=True
    )
    taller = -(-(share + LOSS_PIECES) // 16) * 16
    pieces, *field = lax.optimization_barrier((pieces, *field))
    message_out = pl.pallas_call(
        share_kernel,
        out_shape=jax.ShapeDtypeStruct((cells, taller, hidden_size), bf16),
        in_specs=[in_vmem] * 2,
        out_specs=in_vmem,
        compiler_params=vmem(4),
        name="share_sum",
    )(pieces, loss)
    message_out, left, right = lax.optimization_barrier((message_out, left, right))
    if early < groups:
        field = (solve(groups - 1, left, right, field),)
    final_field = field[0].reshape(init_field.shape)
    gathered = lax.all_to_all(message_out, ("row", "col"), 0, 0, tiled=True)
    gathered, final_field = lax.optimization_barrier((gathered, final_field))
    swap = [(i, (i + 1) % run_size) for i in range(run_size)]
    other = lax.ppermute(gathered, "run", swap)
    cells_total = rows_dev * row_size * wide
    new_w_in, new_bias, new_w_out, mean_loss = pl.pallas_call(
        functools.partial(finish_kernel, share, 1.0 / (rows_all * cells_total)),
        out_shape=(
            jax.ShapeDtypeStruct((inputs, hidden_size), f32),
            jax.ShapeDtypeStruct((1, hidden_size), f32),
            jax.ShapeDtypeStruct((hidden_size, hidden_size), f32),
            jax.ShapeDtypeStruct((1, LANES), f32),
        ),
        in_specs=[in_vmem] * 8,
        out_specs=(in_vmem,) * 4,
        scratch_shapes=[
            pltpu.VMEM((rows_all, hidden_size), bf16),
            pltpu.VMEM((run_size, hidden_size), f32),
        ],
        compiler_params=vmem(12),
        name="trunk_update",
    )(gathered, other, act, slope, rows_in, w_in, bias_in[None], w_out)
    return (final_field, new_w_in, new_bias[0], new_w_out, mean_loss[0, 0])


def solution(mesh):
    in_specs = (
        P("run", "row", "col"),
        P("row", "col"),
        P("run"),
        P("run"),
        P(),
        P(),
        P(),
        P(),
        P(),
        P(None, ("row", "col"), None),
    )
    out_specs = (P("run", "row", "col"), P(), P(), P(), P())
    return jax.shard_map(
        per_device, mesh=mesh, in_specs=in_specs, out_specs=out_specs, check_vma=False
    )
```

```python
import functools
import math

import jax
import jax.numpy as jnp
import numpy as np
from jax import lax
from jax.experimental import pallas as pl
from jax.experimental.pallas import tpu as pltpu
from jax.sharding import PartitionSpec as P

time_step = 0.12
learn_rate = 0.5
LANES = 128
FRONT_PARTS = 2
SUB = 8
GROUP = 16
f32 = jnp.float32
bf16 = jnp.bfloat16


def neighbours(up, down, axis):
    count = lax.axis_size(axis)
    forward = [(i, i + 1) for i in range(count - 1)]
    backward = [(target, source) for source, target in forward]
    return lax.ppermute(up, axis, forward), lax.ppermute(down, axis, backward)


def kappa_of(u, cond, inverse):
    return cond * pltpu.reciprocal(inverse + u * u, approx=True)


def spread(ref, first, count):
    at = lax.broadcasted_iota(jnp.int32, (count, LANES), 0)
    value = jnp.full((count, LANES), ref[first])
    for i in range(1, count):
        value = jnp.where(at == i, ref[first + i], value)
    return value


def apart(wide):
    parts = wide // LANES
    source = np.arange(wide)[:, None]
    place = np.arange(wide)[None, :]
    return jnp.asarray(source == parts * (place % LANES) + place // LANES, bf16)


def reorder(source, target, size, d_ref, order_ref, out_ref, wide_ref):
    _, band, wide = d_ref.shape
    here = pl.ds(pl.multiple_of(target * size, size), size)
    x = d_ref[pl.ds(pl.multiple_of(source * size, size), size)]
    if band % 16:
        x = x.astype(f32).reshape(size * band, wide).astype(bf16)
    else:
        x = x.reshape(size * band, wide)
    y = jnp.dot(x, order_ref[...], preferred_element_type=f32)
    for part in range(wide // LANES):
        wide_ref[part] = y[:, part * LANES : (part + 1) * LANES]
    for row in range(band):
        for part in range(wide // LANES):
            lanes = pl.ds(row * wide + part * LANES, LANES)
            out_ref[here, lanes] = wide_ref[part, pl.ds(row, size, stride=band), :].astype(bf16)


def product(left_ref, right_ref):
    cells = left_ref.shape[1]
    size = min(cells, 2048)
    total = None
    for start in range(0, cells, size):
        part = lax.dot_general(
            left_ref[:, start : start + size],
            right_ref[:, start : start + size],
            (((1,), (1,)), ((), ())),
            preferred_element_type=f32,
        )
        total = part if total is None else total + part
    return total


ROW_SEGS = 8
COND_ROWS = 16
COL_SEGS = 16


def tile_order(halo, cols_dev):
    across = (cols_dev + 2 * halo) // COL_SEGS
    lanes = ROW_SEGS * COL_SEGS
    place = np.arange(across * lanes)
    column = (place % COL_SEGS) * across + place // lanes
    seg_row = (place % lanes) // COL_SEGS
    source = np.arange(ROW_SEGS * cols_dev)[:, None]
    main = (source // cols_dev == seg_row) & (source % cols_dev + halo == column)
    half = ROW_SEGS * halo
    parity = np.arange(2)[:, None, None, None]
    high = np.arange(2)[:, None, None]
    source = np.arange(LANES)[:, None]
    edge = (
        (source // half == parity)
        & (source % half // halo == seg_row)
        & (source % halo + high * (cols_dev + halo) == column)
    )
    return jnp.asarray(np.concatenate([main, edge.reshape(4 * LANES, -1)]), bf16)


def row_source(halo, rows_dev, runs, refs):
    x_ref, cond_ref, top_ref, bottom_ref = refs

    def source(row):
        if row < halo:
            return top_ref[pl.ds(row, runs, stride=halo), :], top_ref[pl.ds(runs * halo + row, 1), :]
        row -= halo
        if row < rows_dev:
            return x_ref[pl.ds(row, runs, stride=rows_dev), :], cond_ref[pl.ds(row, 1), :]
        row -= rows_dev
        return (
            bottom_ref[pl.ds(row, runs, stride=halo), :],
            bottom_ref[pl.ds(runs * halo + row, 1), :],
        )

    def both(row, copies):
        runs_of, cond = source(row)
        return jnp.concatenate([runs_of, jnp.broadcast_to(cond, (copies, LANES))], axis=0)

    return both


def pack_kernel(halo, runs, x_ref, cond_ref, top_ref, bottom_ref, low_ref, high_ref):
    rows_dev = cond_ref.shape[0]
    source = row_source(halo, rows_dev, runs, (x_ref, cond_ref, top_ref, bottom_ref))
    deep = (rows_dev + 2 * halo) // ROW_SEGS
    half = ROW_SEGS * halo
    lane = lax.broadcasted_iota(jnp.int32, (runs + SUB, LANES), 1)
    for block in range(low_ref.shape[0]):
        low = jnp.zeros((runs + SUB, LANES), f32)
        high = jnp.zeros((runs + SUB, LANES), f32)
        for parity in range(2):
            if 2 * block + parity >= deep:
                break
            for seg in range(ROW_SEGS):
                value = source(seg * deep + 2 * block + parity, SUB)
                spot = parity * half + seg * halo
                here = (lane >= spot) & (lane < spot + halo)
                first = pltpu.roll(value, spot, 1) if spot else value
                shift = (spot + halo) % LANES
                last = pltpu.roll(value, shift, 1) if shift else value
                low = jnp.where(here, first, low)
                high = jnp.where(here, last, high)
        low_ref[block] = low
        high_ref[block] = high


LOSS_PIECES = 3
PIECES = 2


def pieces_of(x, count=PIECES):
    pieces = []
    for _ in range(count):
        pieces.append(x.astype(bf16))
        x = x - pieces[-1].astype(f32)
    return pieces


def tile_kernel(part, halo, steps, runs, *refs):
    x_ref, cond_ref, top_ref, bottom_ref, left_ref, right_ref, nonlin_ref, counts_ref = refs[:8]
    places_ref = refs[8]
    out_ref, u_ref, c_ref, rate_ref, body_ref, ends_ref, back_ref, pad_ref = refs[-8:]
    rows_dev, cols_dev = cond_ref.shape
    deep = (rows_dev + 2 * halo) // ROW_SEGS
    across = (cols_dev + 2 * halo) // COL_SEGS
    packs = left_ref.shape[0]
    edges = ROW_SEGS * cols_dev
    first_run = part * GROUP
    row_at, row_count = lax.axis_index("row"), lax.axis_size("row")
    col_at, col_count = lax.axis_index("col"), lax.axis_size("col")

    def source(row):
        if row < halo:
            return top_ref[pl.ds(first_run * halo + row, GROUP, stride=halo), :]
        row -= halo
        if row < rows_dev:
            return x_ref[pl.ds(row, GROUP, stride=rows_dev), :]
        return bottom_ref[pl.ds(first_run * halo + row - rows_dev, GROUP, stride=halo), :]

    pad_ref[...] = jnp.zeros_like(pad_ref)
    pad_ref[:halo] = top_ref[runs * halo : (runs + 1) * halo]
    pad_ref[halo : halo + rows_dev] = cond_ref[...]
    pad_ref[halo + rows_dev : 2 * halo + rows_dev] = bottom_ref[runs * halo : (runs + 1) * halo]
    for seg in range(ROW_SEGS):
        lanes = slice(seg * cols_dev, (seg + 1) * cols_dev)
        for b in range(deep):
            for i, piece in enumerate(pieces_of(source(seg * deep + b))):
                body_ref[i, b * GROUP : (b + 1) * GROUP, lanes] = piece
        for i, piece in enumerate(pieces_of(pad_ref[seg * deep : seg * deep + COND_ROWS])):
            body_ref[i, deep * GROUP : deep * GROUP + COND_ROWS, lanes] = piece
    for side, ref in enumerate((left_ref, right_ref)):
        lanes = slice(side * LANES, (side + 1) * LANES)
        for block in range(packs):
            for i, piece in enumerate(pieces_of(ref[block, first_run : first_run + GROUP])):
                ends_ref[i, block * GROUP : (block + 1) * GROUP, lanes] = piece
        conds = [ref[block, runs : runs + 1] for block in range(packs)]
        conds.append(jnp.zeros((COND_ROWS - packs, LANES), f32))
        for i, piece in enumerate(pieces_of(jnp.concatenate(conds, axis=0))):
            ends_ref[i, packs * GROUP : packs * GROUP + COND_ROWS, lanes] = piece

    lane = lax.broadcasted_iota(jnp.int32, (SUB, LANES), 1)
    chunk = 3 if across % 3 == 0 else 1
    for start in range(0, across, chunk):
        lanes = slice(start * LANES, (start + chunk) * LANES)
        total = None
        extra = [None, None]
        for i in range(PIECES):
            more = jnp.dot(body_ref[i], places_ref[:edges, lanes], preferred_element_type=f32)
            total = more if total is None else total + more
            for parity in range(2):
                more = jnp.dot(ends_ref[i], places_ref[edges + 2 * LANES * parity : edges + 2 * LANES * (parity + 1), lanes], preferred_element_type=f32)
                extra[parity] = more if extra[parity] is None else extra[parity] + more
        for b in range(deep):
            first = b // 2 * GROUP
            value = total[b * GROUP : (b + 1) * GROUP] + extra[b % 2][first : first + GROUP]
            at = packs * GROUP + b // 2
            cond = total[deep * GROUP + b : deep * GROUP + b + 1] + extra[b % 2][at : at + 1]
            for inner in range(chunk):
                q = start + inner
                here = slice(inner * LANES, (inner + 1) * LANES)
                u_ref[0, b, q] = value[:, here]
                c_ref[b + 1, q] = jnp.broadcast_to(cond[:, here], (SUB, LANES))
    for b in range(deep):
        for q in range(across):
            row = lane // COL_SEGS * deep + b
            col = lane % COL_SEGS * across + q
            inside = (
                ((row >= halo) | (row_at > 0))
                & ((row < halo + rows_dev) | (row_at < row_count - 1))
                & ((col >= halo) | (col_at > 0))
                & ((col < halo + cols_dev) | (col_at < col_count - 1))
            )
            rate_ref[b, q] = jnp.where(inside, 0.5 * time_step, 0.0)
    for q in range(across):
        c_ref[0, q] = pltpu.roll(c_ref[deep, q], COL_SEGS, 1)
        c_ref[deep + 1, q] = pltpu.roll(c_ref[1, q], LANES - COL_SEGS, 1)

    def group(index, _):
        where = pl.ds(pl.multiple_of(index * SUB, SUB), SUB)
        inverse = 1.0 / spread(nonlin_ref, first_run + index * SUB, SUB)
        counts = spread(counts_ref, first_run + index * SUB, SUB)

        def step(number, old, new):
            active = jnp.where(number < counts, inverse, 0.0)

            def get(b, q):
                if b < 0:
                    u = pltpu.roll(u_ref[old, deep - 1, q, where, :], COL_SEGS, 1)
                elif b == deep:
                    u = pltpu.roll(u_ref[old, 0, q, where, :], LANES - COL_SEGS, 1)
                else:
                    u = u_ref[old, b, q, where, :]
                return u, kappa_of(u, c_ref[b + 1, q], inverse)

            last = [get(-1, q) for q in range(across)]
            here = [get(0, q) for q in range(across)]
            below = [(k0 + k1) * (u1 - u0) for (u0, k0), (u1, k1) in zip(last, here)]
            for b in range(deep):
                u = [pair[0] for pair in here]
                k = [pair[1] for pair in here]
                u.append(pltpu.roll(u[0], LANES - 1, 1))
                k.append(pltpu.roll(k[0], LANES - 1, 1))
                side = [(k[q] + k[q + 1]) * (u[q + 1] - u[q]) for q in range(across)]
                side.append(pltpu.roll(side[across - 1], 1, 1))
                then = [get(b + 1, q) for q in range(across)]
                above = [(k[q] + then[q][1]) * (then[q][0] - u[q]) for q in range(across)]
                for q in range(across):
                    flux = (above[q] - below[q]) + (side[q] - side[q - 1])
                    u_ref[new, b, q, where, :] = u[q] + (rate_ref[b, q] * active) * flux
                here, below = then, above

        def two(i, _):
            step(2 * i, 0, 1)
            step(2 * i + 1, 1, 0)
            return 0

        lax.fori_loop(0, steps // 2, two, 0)
        return 0

    lax.fori_loop(0, GROUP // SUB, group, 0)

    for b in range(deep):
        for q in range(across):
            for i, piece in enumerate(pieces_of(u_ref[0, b, q])):
                back_ref[i, b * GROUP : (b + 1) * GROUP, q * LANES : (q + 1) * LANES] = piece
    chunk = 2 if ROW_SEGS % 2 == 0 else 1
    for start in range(0, ROW_SEGS, chunk):
        places = slice(start * cols_dev, (start + chunk) * cols_dev)
        total = None
        for i in range(PIECES):
            more = lax.dot_general(
                back_ref[i], places_ref[places, :], (((1,), (1,)), ((), ())), preferred_element_type=f32
            )
            total = more if total is None else total + more
        for b in range(deep):
            for inner in range(chunk):
                row = (start + inner) * deep + b - halo
                if 0 <= row < rows_dev:
                    out_ref[pl.ds(row, GROUP, stride=rows_dev), :] = total[
                        b * GROUP : (b + 1) * GROUP, inner * cols_dev : (inner + 1) * cols_dev
                    ]


def decoder_kernel(d_ref, order_ref, out_ref, wide_ref):
    reorder(0, 0, d_ref.shape[0], d_ref, order_ref, out_ref, wide_ref)


def strip_kernel(halo, steps, runs, scale_of, *refs):
    count = lax.axis_size("col")
    blocks = refs[:count]
    order_ref, nonlin_ref, counts_ref, hidden_ref, weights_hbm = refs[count : count + 5]
    out_ref, loss_ref, u_ref, c_ref, turned_ref, wide_ref = refs[count + 5 : count + 11]
    shot_ref, weights_ref, gram_ref, square_ref, sems = refs[count + 11 :]
    cols_dev = blocks[0].shape[2]
    wide = count * cols_dev
    parts = wide // LANES
    rows = u_ref.shape[0]
    band = rows - 2 * halo
    index = pl.program_id(0)
    col_at = lax.axis_index("col")
    row_at, row_count = lax.axis_index("row"), lax.axis_size("row")
    has_top = (row_at > 0) | (col_at > 0)
    has_bottom = (row_at < row_count - 1) | (col_at < count - 1)
    lane = lax.broadcasted_iota(jnp.int32, (GROUP, LANES), 1)
    first_lane, last_lane = lane == 0, lane == LANES - 1

    def ordered(get):
        whole = jnp.concatenate([get(block) for block in blocks], axis=1)
        return jnp.dot(whole, turned_ref[...], preferred_element_type=f32)

    groups = runs // GROUP
    each = -(-band // groups)
    cells = band * wide
    fetches = []
    for part in range(groups):
        lanes = slice(min(part * each * wide, cells), min((part + 1) * each * wide, cells))
        if lanes.start < lanes.stop:
            fetches.append(
                pltpu.make_async_copy(
                    weights_hbm.at[:, lanes], weights_ref.at[:, lanes], sems.at[part]
                )
            )

    @pl.when(index == 0)
    def _():
        for fetch in fetches:
            fetch.start()
        if weights_ref.shape[1] > cells:
            weights_ref[:, cells:] = jnp.zeros_like(weights_ref[:, cells:])
        gram_ref[...] = jnp.zeros_like(gram_ref)
        for back in range(count):
            at = lax.rem(col_at + count - back, count)
            turned_ref[back * cols_dev : (back + 1) * cols_dev, :] = order_ref[
                pl.ds(pl.multiple_of(at * cols_dev, cols_dev), cols_dev), :
            ]
        plane = ordered(lambda block: block[runs])
        for row in range(rows):
            c_ref[row] = jnp.broadcast_to(plane[row : row + 1], (SUB, wide))
        square_ref[...] = jnp.zeros_like(square_ref)

    for part, fetch in enumerate(fetches):
        pl.when(index == part)(fetch.wait)

    def split(x):
        return [x[..., part * LANES : (part + 1) * LANES] for part in range(parts)]

    where = pl.ds(pl.multiple_of(index * GROUP, GROUP), GROUP)
    fields = ordered(lambda block: block[where].reshape(GROUP * rows, cols_dev))
    for part, values in enumerate(split(fields)):
        wide_ref[part] = values
    for row in range(rows):
        for part in range(parts):
            lanes = pl.ds(part * LANES, LANES)
            u_ref[row, :, lanes] = wide_ref[part, pl.ds(row, GROUP, stride=rows), :]
    inverse = 1.0 / spread(nonlin_ref, index * GROUP, GROUP)
    counts = spread(counts_ref, index * GROUP, GROUP)
    first_row = pl.multiple_of(index * GROUP * steps, GROUP)

    def get(row):
        u = split(u_ref[row])
        cond = split(jnp.concatenate([c_ref[row]] * (GROUP // SUB), axis=0))
        return u, [kappa_of(a, b, inverse) for a, b in zip(u, cond)]

    for number in range(steps):
        factor = jnp.where(number < counts, 0.5 * time_step * inverse, 0.0)
        top_scale = jnp.where(has_top, factor, 0.0)
        bottom_scale = jnp.where(has_bottom, factor, 0.0)

        def one(row, carry, scale, keep):
            u, k, below, square = carry
            then_u, then_k = get(row + 1)
            above = [(a + b) * (c - d) for a, b, c, d in zip(k, then_k, then_u, u)]
            u_more = u + [jnp.where(last_lane, 0.0, pltpu.roll(u[0], LANES - 1, 1))]
            k_more = k + [jnp.where(last_lane, 0.0, pltpu.roll(k[0], LANES - 1, 1))]
            side = [(k_more[p] + k_more[p + 1]) * (u_more[p + 1] - u_more[p]) for p in range(parts)]
            start = jnp.where(first_lane, k[0] * u[0], pltpu.roll(side[-1], 1, 1))
            side = [start] + side
            for p in range(parts):
                fresh = u[p] + scale * ((above[p] - below[p]) + (side[p + 1] - side[p]))
                u_ref[row, :, pl.ds(p * LANES, LANES)] = fresh
                if keep:
                    shot = fresh.astype(bf16)
                    lanes = pl.ds((row - halo) * wide + p * LANES, LANES)
                    shot_ref[pl.ds(first_row + number * GROUP, GROUP), lanes] = shot
                    again = shot.astype(f32)
                    square = square + again * again
            return then_u, then_k, above, square

        last_u, last_k = get(number)
        u, k = get(number + 1)
        below = [(a + b) * (c - d) for a, b, c, d in zip(k, last_k, u, last_u)]
        carry = (u, k, below, jnp.zeros((GROUP, LANES), f32))
        for row in range(number + 1, halo):
            carry = one(row, carry, top_scale, False)
        for row in range(halo, halo + band):
            carry = one(row, carry, factor, True)
        for row in range(halo + band, rows - 1 - number):
            carry = one(row, carry, bottom_scale, False)
        square_ref[...] += carry[3]
        half = gram_ref.shape[0] // 2
        for spare in range(each * number // steps, each * (number + 1) // steps):
            lanes = pl.ds(pl.multiple_of((index * each + spare) * wide, wide), wide)
            cell = weights_ref[:, lanes]
            dims = (((1,), (1,)), ((), ()))
            gram_ref[:half] += lax.dot_general(cell[:half], cell, dims, preferred_element_type=f32)
            gram_ref[half:, half:] += lax.dot_general(
                cell[half:], cell[half:], dims, preferred_element_type=f32
            )

    @pl.when(index == pl.num_programs(0) - 1)
    def _():
        size = runs * steps
        hidden = hidden_ref[pl.ds(pl.multiple_of(lax.axis_index("run") * size, size), size), :]
        half = gram_ref.shape[0] // 2
        lower = jnp.concatenate([gram_ref[:half, half:].T, gram_ref[half:, half:]], axis=1)
        pushed = None
        for piece in pieces_of(jnp.concatenate([gram_ref[:half], lower], axis=0)):
            part = jnp.dot(hidden, piece, preferred_element_type=f32)
            pushed = part if pushed is None else pushed + part
        drawn = product(shot_ref, weights_ref)
        out_ref[...] = ((pushed - drawn) * scale_of).astype(bf16)
        loss = jnp.sum(hidden.astype(f32) * (pushed - 2.0 * drawn), axis=0, keepdims=True)
        loss_ref[...] = loss
        loss_ref[:, :LANES] += jnp.sum(square_ref[...], axis=0, keepdims=True)


def share_kernel(pieces_ref, loss_ref, out_ref):
    total = pieces_ref[0].astype(f32)
    for source in range(1, pieces_ref.shape[0]):
        total = total + pieces_ref[source].astype(f32)
    rows = [piece.astype(f32) for piece in pieces_of(loss_ref[...], LOSS_PIECES)]
    filler = jnp.zeros((out_ref.shape[1] - total.shape[0] - LOSS_PIECES, total.shape[1]), f32)
    message = jnp.concatenate([total] + rows + [filler], axis=0).astype(bf16)
    for target in range(out_ref.shape[0]):
        out_ref[target] = message


def finish_kernel(
    share, loss_scale, mine_ref, other_ref, rows_ref, w_in_ref, bias_ref,
    w_out_ref, new_in_ref, new_bias_ref, new_out_ref, loss_ref, grad_ref, parts_ref,
):
    pre = jnp.dot(rows_ref[...], w_in_ref[...], preferred_element_type=f32) + bias_ref[...]
    root, cube = (2.0 / math.pi) ** 0.5, 0.044715
    square = pre * pre
    bend = jnp.tanh(root * pre * (1.0 + cube * square))
    rise = 0.5 + 0.5 * bend
    act = (pre * rise).astype(bf16)
    slope = rise + 0.5 * pre * (1.0 - bend * bend) * (root * (1.0 + 3.0 * cube * square))
    core = lax.axis_index("run")
    cells = mine_ref.shape[0]
    for at, ref in ((core, mine_ref), (1 - core, other_ref)):
        parts = jnp.zeros((1, ref.shape[2]), f32)
        rows = []
        for source in range(cells):
            value = ref[source].astype(f32)
            rows.append(value[:share])
            for piece in range(LOSS_PIECES):
                parts = parts + value[share + piece : share + piece + 1]
        size = cells * share
        grad_ref[pl.ds(pl.multiple_of(at * size, size), size), :] = jnp.concatenate(
            rows, axis=0
        ).astype(bf16)
        parts_ref[pl.ds(at, 1), :] = parts
    loss = jnp.sum(parts_ref[0:1] + parts_ref[1:2], axis=1, keepdims=True) * loss_scale
    loss_ref[...] = jnp.broadcast_to(loss, loss_ref.shape)
    grad = grad_ref[...]
    by_rows = (((0,), (0,)), ((), ()))
    grad_out = lax.dot_general(act, grad, by_rows, preferred_element_type=f32)
    new_out_ref[...] = w_out_ref[...].astype(f32) - learn_rate * grad_out
    back = lax.dot_general(
        grad, w_out_ref[...], (((1,), (1,)), ((), ())), preferred_element_type=f32
    )
    grad_pre = back * slope
    new_bias_ref[...] = bias_ref[...] - learn_rate * jnp.sum(grad_pre, axis=0, keepdims=True)
    grad_in = lax.dot_general(
        rows_ref[...], grad_pre.astype(bf16), by_rows, preferred_element_type=f32
    )
    new_in_ref[...] = w_in_ref[...].astype(f32) - learn_rate * grad_in


def per_device(
    init_field, conduct, nonlin, counts, descriptors, time_code, w_in, bias_in, w_out, decoder
):
    runs, rows_dev, cols_dev = init_field.shape
    steps = time_code.shape[0]
    inputs, hidden_size = w_in.shape
    run_size = lax.axis_size("run")
    row_size = lax.axis_size("row")
    col_size = lax.axis_size("col")
    halo = steps
    band = rows_dev // col_size
    rows_strip = band + 2 * halo
    wide = cols_dev * col_size
    groups = runs // GROUP
    runs_total = runs * run_size
    rows_all = runs_total * steps
    scale_of = 1.0 / rows_all

    def vmem(mib):
        return pltpu.CompilerParams(vmem_limit_bytes=mib * 1024 * 1024)

    in_vmem = pl.BlockSpec(memory_space=pltpu.VMEM)
    in_hbm = pl.BlockSpec(memory_space=pltpu.HBM)
    in_smem = pl.BlockSpec(memory_space=pltpu.SMEM)

    tile = jnp.concatenate([init_field, conduct[None]], axis=0)
    top, bottom = neighbours(tile[:, rows_dev - halo :], tile[:, :halo], "row")

    padded = jnp.concatenate([top, tile, bottom], axis=1).astype(bf16)
    col_at = lax.axis_index("col")

    def message(target):
        return lax.dynamic_slice_in_dim(padded, target * band, rows_strip, 1)

    messages = [message((col_at + hop) % col_size) for hop in range(col_size)]

    deep = (rows_dev + 2 * halo) // ROW_SEGS
    across = (cols_dev + 2 * halo) // COL_SEGS
    tile_args = (
        init_field.reshape(runs * rows_dev, cols_dev),
        conduct,
        top.reshape(-1, cols_dev),
        bottom.reshape(-1, cols_dev),
    )
    pack_shape = jax.ShapeDtypeStruct((-(-deep // 2), runs + SUB, LANES), f32)
    low, high = pl.pallas_call(
        functools.partial(pack_kernel, halo, runs),
        out_shape=(pack_shape, pack_shape),
        in_specs=[in_vmem] * 4,
        out_specs=(in_vmem, in_vmem),
        compiler_params=vmem(6),
        name="pack_columns",
    )(*tile_args)
    order = apart(wide)
    (low, high, order), messages = lax.optimization_barrier(((low, high, order), messages))
    left, right = neighbours(high, low, "col")
    blocks = messages[:1]
    for hop in range(1, col_size):
        pairs = [(i, (i + hop) % col_size) for i in range(col_size)]
        blocks.append(lax.ppermute(messages[hop], "col", pairs))

    size = 128
    weights = pl.pallas_call(
        decoder_kernel,
        grid=(hidden_size // size,),
        out_shape=jax.ShapeDtypeStruct((hidden_size, band * wide), bf16),
        in_specs=[pl.BlockSpec((size, band, wide), lambda i: (i, 0, 0)), in_vmem],
        out_specs=pl.BlockSpec((size, band * wide), lambda i: (i, 0)),
        scratch_shapes=[pltpu.VMEM((wide // LANES, size * band, LANES), f32)],
        compiler_params=vmem(20),
        cost_estimate=pl.CostEstimate(flops=10**10, bytes_accessed=10**7, transcendentals=0),
        name="decoder_order",
    )(decoder, order)

    places = tile_order(halo, cols_dev)

    def solve(part, left, right, done):
        block = pl.BlockSpec((GROUP * rows_dev, cols_dev), lambda i: (part, 0))
        packs = left.shape[0]
        return pl.pallas_call(
            functools.partial(tile_kernel, part, halo, steps, runs),
            grid=(1,),
            out_shape=jax.ShapeDtypeStruct((runs * rows_dev, cols_dev), f32),
            in_specs=[block] + [in_vmem] * 5 + [in_smem] * 2 + [in_vmem] + [in_hbm] * len(done),
            out_specs=block,
            scratch_shapes=[
                pltpu.VMEM((2, deep, across, GROUP, LANES), f32),
                pltpu.VMEM((deep + 2, across, SUB, LANES), f32),
                pltpu.VMEM((deep, across, SUB, LANES), f32),
                pltpu.VMEM((PIECES, deep * GROUP + COND_ROWS, ROW_SEGS * cols_dev), bf16),
                pltpu.VMEM((PIECES, packs * GROUP + COND_ROWS, 2 * LANES), bf16),
                pltpu.VMEM((PIECES, deep * GROUP, across * LANES), bf16),
                pltpu.VMEM((rows_dev + 2 * halo + COND_ROWS, cols_dev), f32),
            ],
            input_output_aliases={9: 0} if done else {},
            compiler_params=vmem(14),
            cost_estimate=pl.CostEstimate(
                flops=10**10 if done else 10**11, bytes_accessed=10**7, transcendentals=0
            ),
            name="tile_solver",
        )(*tile_args, left, right, nonlin, counts, places, *done)

    early = FRONT_PARTS
    field = ()
    for part in range(early):
        field = (solve(part, left, right, field),)

    desc = descriptors.astype(f32).reshape(run_size * groups, 1, GROUP, -1)
    codes = time_code.astype(f32)[None, :, None, :]
    rows_in = (desc + codes).astype(bf16).reshape(rows_all, -1)
    pre = jnp.dot(rows_in, w_in, preferred_element_type=f32) + bias_in
    act = jax.nn.gelu(pre).astype(bf16)
    hidden = jnp.dot(act, w_out, preferred_element_type=f32).astype(bf16)
    hidden, *field = lax.optimization_barrier((hidden, *field))
    partial, loss = pl.pallas_call(
        functools.partial(strip_kernel, halo, steps, runs, scale_of),
        grid=(groups,),
        out_shape=(
            jax.ShapeDtypeStruct((runs * steps, hidden_size), bf16),
            jax.ShapeDtypeStruct((1, hidden_size), f32),
        ),
        in_specs=[in_vmem] * (col_size + 1) + [in_smem] * 2 + [in_vmem, in_hbm],
        out_specs=(in_vmem, in_vmem),
        scratch_shapes=[
            pltpu.VMEM((rows_strip, GROUP, wide), f32),
            pltpu.VMEM((rows_strip, SUB, wide), f32),
            pltpu.VMEM((wide, wide), bf16),
            pltpu.VMEM((wide // LANES, GROUP * rows_strip, LANES), f32),
            pltpu.VMEM((runs * steps, band * wide), bf16),
            pltpu.VMEM((hidden_size, -(-band // groups) * groups * wide), bf16),
            pltpu.VMEM((hidden_size, hidden_size), f32),
            pltpu.VMEM((GROUP, LANES), f32),
            pltpu.SemaphoreType.DMA((groups,)),
        ],
        compiler_params=vmem(30),
        name="strip_solver",
    )(*blocks, order, nonlin, counts, hidden, weights)

    cells = row_size * col_size
    share = runs * steps // cells
    partial, left, right = lax.optimization_barrier((partial, left, right))
    for part in range(early, groups - 1):
        field = (solve(part, left, right, field),)
    pieces = lax.all_to_all(
        partial.reshape(cells, share, hidden_size), ("row", "col"), 0, 0, tiled=True
    )
    taller = -(-(share + LOSS_PIECES) // 16) * 16
    pieces, *field = lax.optimization_barrier((pieces, *field))
    message_out = pl.pallas_call(
        share_kernel,
        out_shape=jax.ShapeDtypeStruct((cells, taller, hidden_size), bf16),
        in_specs=[in_vmem] * 2,
        out_specs=in_vmem,
        compiler_params=vmem(4),
        name="share_sum",
    )(pieces, loss)
    message_out, left, right = lax.optimization_barrier((message_out, left, right))
    if early < groups:
        field = (solve(groups - 1, left, right, field),)
    final_field = field[0].reshape(init_field.shape)
    gathered = lax.all_to_all(message_out, ("row", "col"), 0, 0, tiled=True)
    gathered, final_field = lax.optimization_barrier((gathered, final_field))
    swap = [(i, (i + 1) % run_size) for i in range(run_size)]
    other = lax.ppermute(gathered, "run", swap)
    cells_total = rows_dev * row_size * wide
    new_w_in, new_bias, new_w_out, mean_loss = pl.pallas_call(
        functools.partial(finish_kernel, share, 1.0 / (rows_all * cells_total)),
        out_shape=(
            jax.ShapeDtypeStruct((inputs, hidden_size), f32),
            jax.ShapeDtypeStruct((1, hidden_size), f32),
            jax.ShapeDtypeStruct((hidden_size, hidden_size), f32),
            jax.ShapeDtypeStruct((1, LANES), f32),
        ),
        in_specs=[in_vmem] * 6,
        out_specs=(in_vmem,) * 4,
        scratch_shapes=[
            pltpu.VMEM((rows_all, hidden_size), bf16),
            pltpu.VMEM((run_size, hidden_size), f32),
        ],
        compiler_params=vmem(20),
        name="trunk_update",
    )(gathered, other, rows_in, w_in, bias_in[None], w_out)
    return (final_field, new_w_in, new_bias[0], new_w_out, mean_loss[0, 0])


def solution(mesh):
    in_specs = (
        P("run", "row", "col"),
        P("row", "col"),
        P("run"),
        P("run"),
        P(),
        P(),
        P(),
        P(),
        P(),
        P(None, ("row", "col"), None),
    )
    out_specs = (P("run", "row", "col"), P(), P(), P(), P())
    return jax.shard_map(
        per_device, mesh=mesh, in_specs=in_specs, out_specs=out_specs, check_vma=False
    )
```
